32 devices in a mesh: dp: 2 (over y), fsdp: 16 (over z, x, core).
Axes of the slice: x: 2, y: 2, z: 4, core: 2. Of those that a mesh axis runs over, the one named last changes fastest.
Arguments:
- acts: bfloat16 [14336, 7168], P(('dp', 'fsdp')), may hold values from -6 to 6
- upstream: bfloat16 [14336, 512], P(('dp', 'fsdp')), may hold values from -1.25 to 1.25
- k_weight: bfloat16 [7168, 512], P('fsdp'), may hold values from -0.0625 to 0.0625
- probe: bfloat16 [7168, 512], P('fsdp'), may hold values from -5 to 5
- norm_gain: float32 [128], replicated, may hold values from 0.1 to 1.9
- momentum: float32 [7168, 512], P('fsdp', 'dp'), may hold values from -4 to 4
- curvature: float32 [7168, 512], P('fsdp', 'dp'), may hold values from 0.3 to 3
Outputs:
- new_momentum: float32 [7168, 512], P('fsdp', 'dp')
- new_curvature: float32 [7168, 512], P('fsdp', 'dp')
- update: float32 [7168, 512], P('fsdp', 'dp')
The draws below stay inside these ranges and needn't reach their ends.
All inputs are finite; a program needn't handle non-finite values.
Results may differ from the reference program's by a relative error of at most 0.024.
Values may be sent and summed in bfloat16 or wider, within the bound.
No kernel may reach another device: no remote copies, remote signals or barrier semaphores. Data moves between devices by JAX's collectives and lax.ppermute only.
A program may use at most 128 MiB of HBM per device.

```python
import math
import jax
import jax.numpy as jnp
from jax import lax

D = 7168
HEAD_DIM = 128
TOK_DEV = 448
KV_WIDTH = 512
TOKENS = 14336


def strengthened(drawn, rng, source, target, blocks, factor):
    def block_of(position):
        return (jnp.arange(drawn.shape[position]) // (drawn.shape[position] // blocks)).reshape((-1,) + (1,) * (drawn.ndim - 1 - position))

    one_side = jax.random.permutation(rng, blocks)[block_of(target)]
    far = (block_of(target) + blocks // 2) % blocks
    return jnp.where((block_of(source) == one_side) | (block_of(source) == far), factor * drawn, drawn)


def block_levels(stream_key, extent, split, smallest, top_value):
    gain = 1.0
    for dim, shards_of in split:
        draws = jax.random.uniform(jax.random.fold_in(jax.random.fold_in(stream_key, 6), dim), (shards_of,), jnp.float32, smallest / len(split), top_value / len(split))
        gain = gain * jnp.repeat(jnp.exp(draws), extent[dim] // shards_of).reshape((-1,) + (1,) * (len(extent) - 1 - dim))
    return gain


def gaussian(stream_key, shape, deviation, bound, cuts=(), held_as=jnp.bfloat16):
    factor_of = block_levels(stream_key, shape, cuts, -0.22, 0.18) if cuts else 1.0
    result = jax.random.normal(stream_key, shape, jnp.float32) * deviation * factor_of
    return jnp.minimum(jnp.maximum(result, -bound), bound).astype(held_as)


def gaussian_with(own_key, dims, scale, reach, split, heavy, held_as=jnp.bfloat16):
    result = scale * jax.random.normal(own_key, dims, jnp.float32)
    if split:
        result = result * block_levels(own_key, dims, split, -0.22, 0.18)
    return jnp.clip(strengthened(result, jax.random.fold_in(own_key, 3), *heavy), -reach, reach).astype(held_as)


def setup_inputs(seed: int = 0) -> dict:
    splits = jax.random.split(jax.random.key(seed), 8)
    acts = gaussian_with(splits[0], (TOKENS, D), 1.0, 6.0, ((0, 32),), (0, 1, 32, 2.75))
    upstream = gaussian(splits[1], (TOKENS, KV_WIDTH), (10 * TOKENS ** -0.5), 1.25, ((0, 32),))
    k_weight = gaussian(splits[2], (D, KV_WIDTH), D ** -0.5, 0.0625, ((0, 16),))
    probe = gaussian(splits[3], (D, KV_WIDTH), 1.0, 5.0, ((0, 16),))
    norm_gain = jnp.clip(1.0 + 0.18 * jax.random.normal(splits[4], (HEAD_DIM,), jnp.float32), 0.1, 1.9)
    momentum = gaussian(splits[5], (D, KV_WIDTH), 0.3, 4.0, ((0, 16), (1, 2)), jnp.float32)
    curvature = jnp.clip(jnp.exp(math.log(3.0) - 2.3025851 * jax.random.uniform(splits[6], (D, KV_WIDTH), jnp.float32) ** block_levels(splits[6], (D, KV_WIDTH), ((0, 16), (1, 2)), -0.2, 0.2)), 0.3, 3.0)
    return {"acts": acts, "upstream": upstream, "k_weight": k_weight, "probe": probe, "norm_gain": norm_gain, "momentum": momentum, "curvature": curvature}


def head_terms(projected, tangent, upstream, norm_gain):
    token_count = projected.shape[0]
    head_size = norm_gain.shape[0]
    head_count = projected.shape[1] // head_size
    shaped = (token_count, head_count, head_size)
    values = projected.reshape(shaped)
    moving = tangent.reshape(shaped)
    weighted = upstream.astype(jnp.float32).reshape(shaped) * norm_gain
    inverse = lax.rsqrt(lax.optimization_barrier(jnp.mean(values * values, axis=-1, keepdims=True)) + 1e-06)
    cubed = inverse * inverse * inverse
    along = lax.optimization_barrier(jnp.sum(weighted * values, axis=-1, keepdims=True))
    grad_vals = inverse * weighted - cubed * values * along / head_size
    inverse_dot = -cubed * lax.optimization_barrier(jnp.sum(values * moving, axis=-1, keepdims=True)) / head_size
    along_dot = lax.optimization_barrier(jnp.sum(weighted * moving, axis=-1, keepdims=True))
    hvp_vals = inverse_dot * weighted - (3.0 * inverse * inverse * inverse_dot * values * along + cubed * moving * along + cubed * values * along_dot) / head_size
    return (grad_vals.reshape(token_count, -1), hvp_vals.reshape(token_count, -1))

def reference(acts, upstream, k_weight, probe, norm_gain, momentum, curvature):
    width = k_weight.shape[1]
    model_width = acts.shape[1]

    def block_step(carry, pieces):
        act_rows, cot_rows = pieces
        projected = jnp.dot(act_rows, k_weight, preferred_element_type=jnp.float32)
        tangent = jnp.dot(act_rows, probe, preferred_element_type=jnp.float32)
        grad_vals, hvp_vals = head_terms(projected, tangent, cot_rows, norm_gain)
        stacked = jnp.concatenate([grad_vals, hvp_vals], axis=1).astype(jnp.bfloat16)
        partial_sum = lax.dot_general(act_rows, stacked, (((0,), (0,)), ((), ())), preferred_element_type=jnp.float32)
        rounded = lax.optimization_barrier(partial_sum.astype(jnp.bfloat16))
        return (carry + rounded.astype(jnp.float32), None)
    blocks = acts.reshape(-1, TOK_DEV, model_width)
    cot_blocks = upstream.reshape(-1, TOK_DEV, width)
    total, unused = lax.scan(block_step, jnp.zeros((model_width, 2 * width), jnp.float32), (blocks, cot_blocks))
    gradient = total[:, :width]
    hvp = total[:, width:]
    new_momentum = 0.965 * momentum + 0.035 * gradient
    new_curvature = 0.99 * curvature + 0.01 * (probe.astype(jnp.float32) * hvp)
    update = jnp.clip(new_momentum / jnp.maximum(0.5 * new_curvature, 0.25), -1.0, 1.0)
    return (new_momentum, new_curvature, update)
```

```python
import functools

import jax
import jax.numpy as jnp
from jax import lax
from jax.sharding import PartitionSpec as P

AXES = ("dp", "fsdp")


def contract_tokens(left, right):
    return lax.dot_general(
        left, right, (((0,), (0,)), ((), ())), preferred_element_type=jnp.float32
    )


def head_terms(values, moving, weighted):
    head_size = values.shape[-1]
    inverse = lax.rsqrt(jnp.mean(values * values, axis=-1, keepdims=True) + 1e-06)
    cubed = inverse * inverse * inverse
    along = jnp.sum(weighted * values, axis=-1, keepdims=True)
    grad_vals = inverse * weighted - cubed * values * along / head_size
    inverse_dot = -cubed * jnp.sum(values * moving, axis=-1, keepdims=True) / head_size
    along_dot = jnp.sum(weighted * moving, axis=-1, keepdims=True)
    hvp_vals = (
        inverse_dot * weighted
        - (
            3.0 * inverse * inverse * inverse_dot * values * along
            + cubed * moving * along
            + cubed * values * along_dot
        )
        / head_size
    )
    return grad_vals, hvp_vals


def step_outputs(momentum, curvature, probe_cols, grad_share, hvp_share):
    new_momentum = 0.965 * momentum + 0.035 * grad_share
    new_curvature = 0.99 * curvature + 0.01 * (probe_cols * hvp_share)
    update = jnp.clip(new_momentum / jnp.maximum(0.5 * new_curvature, 0.25), -1.0, 1.0)
    return (new_momentum, new_curvature, update)


def by_collectives(acts, upstream, k_weight, probe, norm_gain, momentum, curvature):
    width = k_weight.shape[1]
    weight_piece = lax.all_gather(k_weight, "fsdp", axis=0, tiled=True)
    probe_piece = lax.all_gather(probe, "fsdp", axis=0, tiled=True)
    projected = jnp.dot(acts, weight_piece, preferred_element_type=jnp.float32)
    tangent = jnp.dot(acts, probe_piece, preferred_element_type=jnp.float32)
    shaped = (acts.shape[0], -1, norm_gain.shape[0])
    weighted = upstream.astype(jnp.float32).reshape(shaped) * norm_gain
    pair = head_terms(projected.reshape(shaped), tangent.reshape(shaped), weighted)
    stacked = jnp.concatenate([v.reshape(acts.shape[0], -1) for v in pair], axis=1)
    owned = lax.psum_scatter(
        contract_tokens(acts, stacked.astype(jnp.bfloat16)).astype(jnp.bfloat16),
        "fsdp",
        scatter_dimension=0,
        tiled=True,
    ).astype(jnp.float32)
    grad_share, hvp_share = (
        lax.psum_scatter(owned[:, :width], "dp", scatter_dimension=1, tiled=True),
        lax.psum_scatter(owned[:, width:], "dp", scatter_dimension=1, tiled=True),
    )
    share_width = grad_share.shape[1]
    probe_cols = lax.dynamic_slice_in_dim(
        probe, lax.axis_index("dp") * share_width, share_width, 1
    ).astype(jnp.float32)
    return step_outputs(momentum, curvature, probe_cols, grad_share, hvp_share)


def pairs_of(move):
    def flat(y, z, x, c):
        return ((y * 4 + z) * 2 + x) * 2 + c

    found = []
    for y in range(2):
        for z in range(4):
            for x in range(2):
                for c in range(2):
                    target = move(y, z, x, c)
                    if target is not None:
                        found.append((flat(y, z, x, c), flat(*target)))
    return found


def send(value, move):
    return lax.ppermute(value, AXES, pairs_of(move))


def to_core(y, z, x, c):
    return (y, z, x, 1 - c)


def to_x(y, z, x, c):
    return (y, z, 1 - x, c)


def to_y(y, z, x, c):
    return (1 - y, z, x, c)


def to_first(y, z, x, c):
    return to_x(y, z, x, c) if c == 0 else to_y(y, z, x, c)


def to_second(y, z, x, c):
    return to_y(y, z, x, c) if c == 0 else to_x(y, z, x, c)


def to_z(steps):
    return lambda y, z, x, c: (y, steps[z], x, c) if z in steps else None


Z_PAIR = to_z({0: 1, 1: 0, 2: 3, 3: 2})
Z_MIDDLE = to_z({1: 2, 2: 1})
Z_OUT = to_z({1: 0, 2: 3})
Z_IN = to_z({0: 1, 3: 2})


def by_links(acts, upstream, k_weight, probe, norm_gain, momentum, curvature):
    head = norm_gain.shape[0]
    rows = k_weight.shape[0]
    place = lax.axis_index("fsdp")
    y, z, x, c = lax.axis_index("dp"), place // 4, (place // 2) % 2, place % 2
    own_first = c == 0

    def column(value, number):
        return lax.dynamic_slice_in_dim(value, number * head, head, 1)

    def weights_for(core, side):
        return [column(k_weight, 2 * side + core), column(probe, 2 * side + core)]

    leaving = jnp.concatenate(weights_for(1 - c, y) + weights_for(1 - c, 1 - y), axis=1)
    staying = jnp.concatenate(weights_for(c, y) + weights_for(c, 1 - y), axis=1)
    coming = send(leaving, to_core)
    other_acts = send(acts, to_core)
    other_up = send(
        jnp.concatenate(
            [column(upstream, 2 * y + 1 - c), column(upstream, 2 * (1 - y) + 1 - c)], axis=1
        ),
        to_core,
    )
    chip_rows = jnp.where(
        own_first,
        jnp.concatenate([staying, coming], axis=0),
        jnp.concatenate([coming, staying], axis=0),
    )
    mine, beside = chip_rows[:, : 2 * head], chip_rows[:, 2 * head :]

    one = send(mine, Z_PAIR)
    near = send(mine, Z_MIDDLE)
    two = send(near, Z_OUT) + send(one, Z_MIDDLE)
    three = near + send(two, Z_OUT)

    across = send(mine, to_x)
    units = [(mine, across, beside, send(across, to_y))]
    for held in (one, two, three):
        first = send(held, to_first)
        units.append((held, first, send(held, to_second), send(first, to_second)))

    all_acts = jnp.concatenate([acts, other_acts], axis=0)

    def block_of(slot, flip_x):
        start = ((z ^ slot) * 2 + (x ^ flip_x)) * (2 * rows)
        return lax.dynamic_slice_in_dim(all_acts, start, 2 * rows, 1)

    def dot(left, right):
        return jnp.dot(left, right, preferred_element_type=jnp.float32)

    here = there = None
    for slot in range(4):
        own, first, second, both = units[slot]
        if slot == 0:
            flip_y, flip_x = second, first
        else:
            flip_x = jnp.where(own_first, first, second)
            flip_y = jnp.where(own_first, second, first)
        near_x, far_x = block_of(slot, 0), block_of(slot, 1)
        a = dot(near_x, own) + dot(far_x, flip_x)
        b = dot(near_x, flip_y) + dot(far_x, both)
        here = a if here is None else here + a
        there = b if there is None else there + b

    def stacked(projections, side, other):
        weighted = (
            jnp.concatenate([column(upstream, 2 * side + c), other], axis=0).astype(jnp.float32)
            * norm_gain
        )
        pair = head_terms(projections[:, :head], projections[:, head:], weighted)
        return jnp.concatenate(pair, axis=1).astype(jnp.bfloat16)

    right_here = stacked(here, y, other_up[:, :head])
    right_there = stacked(there, 1 - y, other_up[:, head:])
    right_first = jnp.where(own_first, right_here, right_there)
    right_second = jnp.where(own_first, right_there, right_here)

    def partial(slot, flip_x, right):
        return contract_tokens(block_of(slot, flip_x), right).astype(jnp.bfloat16)

    def plus(*terms):
        total = terms[0].astype(jnp.float32)
        for term in terms[1:]:
            total = total + term.astype(jnp.float32)
        return total.astype(jnp.bfloat16)

    def over_plane(slot):
        far = partial(slot, 1, right_there)
        second = partial(slot, c, right_second)
        first = partial(slot, 1 - c, right_first)
        own = partial(slot, 0, right_here)
        first = plus(first, send(far, to_second))
        return own, send(second, to_second), send(first, to_first)

    three = plus(*over_plane(3))
    two = plus(*over_plane(2), send(three, Z_IN))
    three = plus(three, send(two, Z_IN))
    one = plus(*over_plane(1), send(two, Z_MIDDLE))
    owned = over_plane(0) + (send(three, Z_MIDDLE), send(one, Z_PAIR))
    owned = functools.reduce(lambda s, t: s + t.astype(jnp.float32), owned, jnp.float32(0))

    kept = lax.dynamic_slice_in_dim(owned, c * rows, rows, 0)
    given = lax.dynamic_slice_in_dim(owned, (1 - c) * rows, rows, 0)
    taken = send(given, to_core)
    left = jnp.where(own_first, kept, taken)
    right = jnp.where(own_first, taken, kept)
    grad_share = jnp.concatenate([left[:, :head], right[:, :head]], axis=1)
    hvp_share = jnp.concatenate([left[:, head:], right[:, head:]], axis=1)
    probe_cols = lax.dynamic_slice_in_dim(probe, y * 2 * head, 2 * head, 1).astype(jnp.float32)
    return step_outputs(momentum, curvature, probe_cols, grad_share, hvp_share)


def solution(mesh):
    on_links = mesh.shape["dp"] == 2 and mesh.shape["fsdp"] == 16
    return jax.shard_map(
        by_links if on_links else by_collectives,
        mesh=mesh,
        in_specs=(
            P(("dp", "fsdp"), None),
            P(("dp", "fsdp"), None),
            P("fsdp", None),
            P("fsdp", None),
            P(),
            P("fsdp", "dp"),
            P("fsdp", "dp"),
        ),
        out_specs=(P("fsdp", "dp"), P("fsdp", "dp"), P("fsdp", "dp")),
        check_vma=False,
    )
```

```python
import functools

import jax
import jax.numpy as jnp
from jax import lax
from jax.experimental import pallas as pl
from jax.experimental.pallas import tpu as pltpu
from jax.sharding import PartitionSpec as P

AXES = ("dp", "fsdp")


def contract_tokens(left, right):
    return lax.dot_general(
        left, right, (((0,), (0,)), ((), ())), preferred_element_type=jnp.float32
    )


def head_terms(values, moving, weighted):
    head_size = values.shape[-1]
    inverse = lax.rsqrt(jnp.mean(values * values, axis=-1, keepdims=True) + 1e-06)
    cubed = inverse * inverse * inverse
    along = jnp.sum(weighted * values, axis=-1, keepdims=True)
    grad_vals = inverse * weighted - cubed * values * along / head_size
    inverse_dot = -cubed * jnp.sum(values * moving, axis=-1, keepdims=True) / head_size
    along_dot = jnp.sum(weighted * moving, axis=-1, keepdims=True)
    hvp_vals = (
        inverse_dot * weighted
        - (
            3.0 * inverse * inverse * inverse_dot * values * along
            + cubed * moving * along
            + cubed * values * along_dot
        )
        / head_size
    )
    return grad_vals, hvp_vals


def step_outputs(momentum, curvature, probe_cols, grad_share, hvp_share):
    new_momentum = 0.965 * momentum + 0.035 * grad_share
    new_curvature = 0.99 * curvature + 0.01 * (probe_cols * hvp_share)
    update = jnp.clip(new_momentum / jnp.maximum(0.5 * new_curvature, 0.25), -1.0, 1.0)
    return (new_momentum, new_curvature, update)


def by_collectives(acts, upstream, k_weight, probe, norm_gain, momentum, curvature):
    width = k_weight.shape[1]
    weight_piece = lax.all_gather(k_weight, "fsdp", axis=0, tiled=True)
    probe_piece = lax.all_gather(probe, "fsdp", axis=0, tiled=True)
    projected = jnp.dot(acts, weight_piece, preferred_element_type=jnp.float32)
    tangent = jnp.dot(acts, probe_piece, preferred_element_type=jnp.float32)
    shaped = (acts.shape[0], -1, norm_gain.shape[0])
    weighted = upstream.astype(jnp.float32).reshape(shaped) * norm_gain
    pair = head_terms(projected.reshape(shaped), tangent.reshape(shaped), weighted)
    stacked = jnp.concatenate([v.reshape(acts.shape[0], -1) for v in pair], axis=1)
    owned = lax.psum_scatter(
        contract_tokens(acts, stacked.astype(jnp.bfloat16)).astype(jnp.bfloat16),
        "fsdp",
        scatter_dimension=0,
        tiled=True,
    ).astype(jnp.float32)
    grad_share, hvp_share = (
        lax.psum_scatter(owned[:, :width], "dp", scatter_dimension=1, tiled=True),
        lax.psum_scatter(owned[:, width:], "dp", scatter_dimension=1, tiled=True),
    )
    share_width = grad_share.shape[1]
    probe_cols = lax.dynamic_slice_in_dim(
        probe, lax.axis_index("dp") * share_width, share_width, 1
    ).astype(jnp.float32)
    return step_outputs(momentum, curvature, probe_cols, grad_share, hvp_share)


def pairs_of(move):
    def flat(y, z, x, c):
        return ((y * 4 + z) * 2 + x) * 2 + c

    found = []
    for y in range(2):
        for z in range(4):
            for x in range(2):
                for c in range(2):
                    target = move(y, z, x, c)
                    if target is not None:
                        found.append((flat(y, z, x, c), flat(*target)))
    return found


def send(value, move, name="exchange"):
    with jax.named_scope(name):
        return lax.ppermute(value, AXES, pairs_of(move))


def after(value, *earlier):
    return lax.optimization_barrier((value, *earlier))[0]


class Order:
    def __init__(self, token):
        self.token = token

    def wait(self, *values):
        *values, self.token = lax.optimization_barrier((*values, self.token))
        return values if len(values) > 1 else values[0]

    def run(self, operation, *values):
        *values, self.token = lax.optimization_barrier((*values, self.token))
        return self.wait(operation(*values))


def to_core(y, z, x, c):
    return (y, z, x, 1 - c)


def to_x(y, z, x, c):
    return (y, z, 1 - x, c)


def to_y(y, z, x, c):
    return (1 - y, z, x, c)


def to_first(y, z, x, c):
    return to_x(y, z, x, c) if c == 0 else to_y(y, z, x, c)


def to_second(y, z, x, c):
    return to_y(y, z, x, c) if c == 0 else to_x(y, z, x, c)


def to_corner(y, z, x, c):
    return to_x(y, z, x, c) if c == 0 else to_y(y, z, x, c)


def to_z(steps):
    return lambda y, z, x, c: (y, steps[z], x, c) if z in steps else None


Z_ONE = to_z({0: 1, 1: 0, 2: 3, 3: 2})
Z_IN = to_z({0: 1, 3: 2})
Z_MIDDLE = to_z({1: 2, 2: 1})
Z_OUT = to_z({1: 0, 2: 3})


VMEM = pl.BlockSpec(memory_space=pltpu.VMEM)
SMEM = pl.BlockSpec(memory_space=pltpu.SMEM)


def call(kernel, outs, scalars, *operands, name):
    return pl.pallas_call(
        kernel,
        out_shape=outs,
        in_specs=[SMEM] + [VMEM] * len(operands),
        out_specs=jax.tree.map(lambda _: VMEM, outs),
        cost_estimate=pl.CostEstimate(flops=10**9, bytes_accessed=10**7, transcendentals=0),
        compiler_params=pltpu.CompilerParams(vmem_limit_bytes=24 * 2**20),
        name=name,
    )(jnp.stack(scalars).astype(jnp.int32), *operands)


def dot(left, right):
    return jnp.dot(left, right, preferred_element_type=jnp.float32)


def halves(tokens):
    half = tokens.shape[0] // 2
    return pl.ds(0, half), pl.ds(half, half)


def spread(block, x, core, rights, tokens_ref, got_ref, kept_ref):
    width = rights[0].shape[0] // 2
    depth = got_ref.shape[2]
    own_first = core == 0
    for begin in range(0, depth, 256):
        size = min(256, depth - begin)
        out = pl.ds(begin, size)

        def products(place):
            at = pl.ds(pl.multiple_of((2 * block + place) * depth, 128) + begin, size)
            return sum(
                dot(right[...], tokens_ref[rows, at])
                for right, rows in zip(rights, halves(tokens_ref))
            )

        near, far = products(x), products(1 - x)
        second = jnp.where(own_first, near[width:], far[:width])
        first = jnp.where(own_first, far[:width], near[width:])
        got_ref[0, :, out] = far[width:].astype(jnp.bfloat16)
        got_ref[1, :, out] = second.astype(jnp.bfloat16)
        kept_ref[0, :, out] = first
        kept_ref[1, :, out] = near[:width]


def spread_shapes(width, depth):
    return [
        jax.ShapeDtypeStruct((2, width, depth), jnp.bfloat16),
        jax.ShapeDtypeStruct((2, width, depth), jnp.float32),
    ]


def contract(scalars, depth, tokens, right_a, right_b):
    def kernel(at_ref, tokens_ref, right_a, right_b, got_ref, kept_ref):
        place = at_ref[0], at_ref[1], at_ref[2]
        spread(*place, (right_a, right_b), tokens_ref, got_ref, kept_ref)

    shapes = spread_shapes(right_a.shape[0] // 2, depth)
    return call(kernel, shapes, scalars, tokens, right_a, right_b, name="contract")


def head_gradients(scalars, depth, tokens, sums, own_up, other_up, norm_gain):
    half = tokens.shape[0] // 2
    width = sums[0].shape[1]
    head = norm_gain.shape[0]

    def kernel(
        at_ref, tokens_ref, own_ref, both_ref, first_ref, second_ref, up_a, up_b, gain_ref,
        right_a, right_b, got_ref, kept_ref,
    ):
        gain = gain_ref[...]
        own_first = at_ref[2] == 0
        for part, (up, right) in enumerate(((up_a, right_a), (up_b, right_b))):
            for begin in range(0, half, 128):
                size = min(128, half - begin)
                within = pl.ds(begin, size)
                at = pl.ds(part * half + begin, size)
                weighted = up[within, :].astype(jnp.float32)
                first, second = first_ref[at, :], second_ref[at, :]
                here = own_ref[at, :] + jnp.where(own_first, first, second)
                there = both_ref[at, :] + jnp.where(own_first, second, first)
                for side, product in enumerate((here, there)):
                    pair = head_terms(
                        product[:, :head],
                        product[:, head:],
                        weighted[:, side * head : (side + 1) * head] * gain,
                    )
                    for i, value in enumerate(pair):
                        features = pl.ds((2 * side + i) * head, head)
                        right[features, within] = value.T.astype(jnp.bfloat16)
        place = at_ref[0], at_ref[1], at_ref[2]
        spread(*place, (right_a, right_b), tokens_ref, got_ref, kept_ref)

    return call(
        kernel,
        [jax.ShapeDtypeStruct((2 * width, half), jnp.bfloat16)] * 2 + spread_shapes(width, depth),
        scalars,
        tokens,
        *sums,
        own_up,
        other_up,
        norm_gain.reshape(1, head),
        name="head_gradients",
    )


def by_rows(kept, got, *terms):
    width, depth = terms[0].shape
    terms = (kept, got, *terms)

    def kernel(kept_ref, got_ref, *refs):
        *term_refs, out_ref = refs
        for begin in range(0, depth, 128):
            size = min(128, depth - begin)
            at = pl.ds(begin, size)
            total = kept_ref[1, :, at] + got_ref[1, :, at].astype(jnp.float32)
            for ref in term_refs:
                total += ref[:, at].astype(jnp.float32)
            out_ref[at, :] = total.T

    return pl.pallas_call(
        kernel,
        out_shape=jax.ShapeDtypeStruct((depth, width), jnp.float32),
        in_specs=[VMEM] * len(terms),
        out_specs=VMEM,
        name="by_rows",
    )(*terms)


def by_links(acts, upstream, k_weight, probe, norm_gain, momentum, curvature):
    head = norm_gain.shape[0]
    rows = k_weight.shape[0]
    place = lax.axis_index("fsdp")
    y, z, x, c = lax.axis_index("dp"), place // 4, (place // 2) % 2, place % 2
    own_first = c == 0

    def column(value, number):
        return lax.dynamic_slice_in_dim(value, number * head, head, 1)

    def weights_for(core, side):
        return [column(k_weight, 2 * side + core), column(probe, 2 * side + core)]

    leaving = jnp.concatenate(weights_for(1 - c, y) + weights_for(1 - c, 1 - y), axis=1)
    staying = jnp.concatenate(weights_for(c, y) + weights_for(c, 1 - y), axis=1)
    coming = send(leaving, to_core, "coming")
    def upstream_for(core):
        return jnp.concatenate(
            [column(upstream, 2 * y + core), column(upstream, 2 * (1 - y) + core)], axis=1
        )

    own_up, other_up = upstream_for(c), send(upstream_for(1 - c), to_core, "other_up")
    chip_rows = jnp.where(
        own_first,
        jnp.concatenate([staying, coming], axis=0),
        jnp.concatenate([coming, staying], axis=0),
    )
    mine, beside = chip_rows[:, : 2 * head], chip_rows[:, 2 * head :]

    order = Order(momentum)
    other_acts = send(after(acts, chip_rows), to_core, "other_acts")
    one = send(mine, Z_ONE, "one")
    near = send(mine, Z_MIDDLE, "near")
    across = send(mine, to_x, "across")
    other_up = order.wait(other_up)
    one, near = order.wait(one, near)
    two_out = send(near, Z_OUT, "two_out")
    two_in = send(one, Z_MIDDLE, "two_in")
    other_acts, one = order.wait(other_acts, one)
    one_first = send(one, to_first, "one_first")
    one_second = send(one, to_second, "one_second")
    corner = order.run(lambda a, b: jnp.where(own_first, a, b), beside, across)
    corner = send(corner, to_corner, "corner")
    tokens = order.run(lambda a, b: jnp.concatenate([a, b], axis=0), acts, other_acts)

    def block_of(held, slot, flip_x):
        start = ((z ^ slot) * 2 + (x ^ flip_x)) * (2 * rows)
        return lax.dynamic_slice_in_dim(held, start, 2 * rows, 1)

    def add_product(total, slot, flip_x, unit):
        def product(unit, held, *before):
            found = jnp.dot(block_of(held, slot, flip_x), unit, preferred_element_type=jnp.float32)
            return sum(before, found)

        return order.run(product, unit, tokens, *(() if total is None else (total,)))

    own_sum = add_product(None, 0, 0, mine)
    both_sum = add_product(None, 0, 0, beside)
    own_sum = add_product(own_sum, 0, 1, across)
    two_out, two_in = order.wait(two_out, two_in)
    two = order.run(jnp.add, two_out, two_in)
    three_out = send(two, Z_OUT, "three_out")
    two_first = send(two, to_first, "two_first")
    own_sum = add_product(own_sum, 1, 0, one)
    one_first = order.wait(one_first)
    one_both = send(one_first, to_second, "one_both")
    corner, two = order.wait(corner, two)
    two_second = send(two, to_second, "two_second")
    both_sum = add_product(both_sum, 0, 1, corner)
    first_sum = add_product(None, 1, 1 - c, one_first)
    second_sum = add_product(None, 1, c, one_second)
    own_sum = add_product(own_sum, 2, 0, two)
    three = order.run(jnp.add, near, three_out)
    three_first = send(three, to_first, "three_first")
    three_second = send(three, to_second, "three_second")
    both_sum = add_product(both_sum, 1, 1, one_both)
    two_first = order.wait(two_first)
    two_both = send(two_first, to_second, "two_both")
    first_sum = add_product(first_sum, 2, 1 - c, two_first)
    own_sum = add_product(own_sum, 3, 0, three)
    second_sum = add_product(second_sum, 2, c, two_second)
    three_first = order.wait(three_first)
    three_both = send(three_first, to_second, "three_both")
    first_sum = add_product(first_sum, 3, 1 - c, three_first)
    both_sum = add_product(both_sum, 2, 1, two_both)
    second_sum = add_product(second_sum, 3, c, three_second)
    both_sum = add_product(both_sum, 3, 1, three_both)

    sums = (own_sum, both_sum, first_sum, second_sum)
    right_a, right_b, leaving_3, kept_3 = head_gradients(
        (z ^ 3, x, c), 2 * rows, tokens, sums, own_up, other_up, norm_gain
    )

    def partial(slot):
        def product(*operands):
            return contract((z ^ slot, x, c), 2 * rows, *operands)

        return order.run(product, tokens, right_a, right_b)

    def total_of(*terms):
        return sum((t.astype(jnp.float32) for t in terms[1:]), terms[0].astype(jnp.float32))

    def rounded(part, kept, got, *more):
        def total(kept, got, *more):
            return total_of(kept[part], got[part], *more).astype(jnp.bfloat16)

        return order.run(total, kept, got, *more)

    seconds_3 = send(leaving_3, to_second, "seconds_3")
    leaving_2, kept_2 = partial(2)
    seconds_2 = send(leaving_2, to_second, "seconds_2")
    leaving_1, kept_1 = partial(1)
    seconds_1 = send(leaving_1, to_second, "seconds_1")
    leaving_0, kept_0 = partial(0)
    seconds_0 = send(leaving_0, to_second, "seconds_0")
    first_3 = send(rounded(0, kept_3, seconds_3), to_first, "first_3")
    first_2 = send(rounded(0, kept_2, seconds_2), to_first, "first_2")
    sum_3 = rounded(1, kept_3, seconds_3, first_3)
    three_in = send(sum_3, Z_IN, "three_in")
    first_1 = send(rounded(0, kept_1, seconds_1), to_first, "first_1")
    sum_2 = rounded(1, kept_2, seconds_2, first_2, three_in)
    two_in = send(sum_2, Z_IN, "two_in")
    two = send(sum_2, Z_MIDDLE, "two")
    sum_3 = order.run(lambda *t: total_of(*t).astype(jnp.bfloat16), sum_3, two_in)
    three = send(sum_3, Z_MIDDLE, "three")
    two = order.wait(two)
    one = send(rounded(1, kept_1, seconds_1, first_1, two), Z_ONE, "one")
    first_0 = send(rounded(0, kept_0, seconds_0), to_first, "first_0")
    owned = order.run(by_rows, kept_0, seconds_0, three, first_0, one)

    kept = lax.dynamic_slice_in_dim(owned, c * rows, rows, 0)
    given = lax.dynamic_slice_in_dim(owned, (1 - c) * rows, rows, 0)
    taken = send(given, to_core, "taken")
    left = jnp.where(own_first, kept, taken)
    right = jnp.where(own_first, taken, kept)
    grad_share = jnp.concatenate([left[:, :head], right[:, :head]], axis=1)
    hvp_share = jnp.concatenate([left[:, head:], right[:, head:]], axis=1)
    probe_cols = lax.dynamic_slice_in_dim(probe, y * 2 * head, 2 * head, 1).astype(jnp.float32)
    return step_outputs(order.token, curvature, probe_cols, grad_share, hvp_share)


def solution(mesh):
    on_links = mesh.shape["dp"] == 2 and mesh.shape["fsdp"] == 16
    return jax.shard_map(
        by_links if on_links else by_collectives,
        mesh=mesh,
        in_specs=(
            P(("dp", "fsdp"), None),
            P(("dp", "fsdp"), None),
            P("fsdp", None),
            P("fsdp", None),
            P(),
            P("fsdp", "dp"),
            P("fsdp", "dp"),
        ),
        out_specs=(P("fsdp", "dp"), P("fsdp", "dp"), P("fsdp", "dp")),
        check_vma=False,
    )
```

```python
import functools

import jax
import jax.numpy as jnp
from jax import lax
from jax.experimental import pallas as pl
from jax.experimental.pallas import tpu as pltpu
from jax.sharding import PartitionSpec as P

AXES = ("dp", "fsdp")


def contract_tokens(left, right):
    return lax.dot_general(
        left, right, (((0,), (0,)), ((), ())), preferred_element_type=jnp.float32
    )


def head_terms(values, moving, weighted):
    head_size = values.shape[-1]
    inverse = lax.rsqrt(jnp.mean(values * values, axis=-1, keepdims=True) + 1e-06)
    cubed = inverse * inverse * inverse
    along = jnp.sum(weighted * values, axis=-1, keepdims=True)
    grad_vals = inverse * weighted - cubed * values * along / head_size
    inverse_dot = -cubed * jnp.sum(values * moving, axis=-1, keepdims=True) / head_size
    along_dot = jnp.sum(weighted * moving, axis=-1, keepdims=True)
    hvp_vals = (
        inverse_dot * weighted
        - (
            3.0 * inverse * inverse * inverse_dot * values * along
            + cubed * moving * along
            + cubed * values * along_dot
        )
        / head_size
    )
    return grad_vals, hvp_vals


def step_outputs(momentum, curvature, probe_cols, grad_share, hvp_share):
    new_momentum = 0.965 * momentum + 0.035 * grad_share
    new_curvature = 0.99 * curvature + 0.01 * (probe_cols * hvp_share)
    update = jnp.clip(new_momentum / jnp.maximum(0.5 * new_curvature, 0.25), -1.0, 1.0)
    return (new_momentum, new_curvature, update)


def by_collectives(acts, upstream, k_weight, probe, norm_gain, momentum, curvature):
    width = k_weight.shape[1]
    weight_piece = lax.all_gather(k_weight, "fsdp", axis=0, tiled=True)
    probe_piece = lax.all_gather(probe, "fsdp", axis=0, tiled=True)
    projected = jnp.dot(acts, weight_piece, preferred_element_type=jnp.float32)
    tangent = jnp.dot(acts, probe_piece, preferred_element_type=jnp.float32)
    shaped = (acts.shape[0], -1, norm_gain.shape[0])
    weighted = upstream.astype(jnp.float32).reshape(shaped) * norm_gain
    pair = head_terms(projected.reshape(shaped), tangent.reshape(shaped), weighted)
    stacked = jnp.concatenate([v.reshape(acts.shape[0], -1) for v in pair], axis=1)
    owned = lax.psum_scatter(
        contract_tokens(acts, stacked.astype(jnp.bfloat16)).astype(jnp.bfloat16),
        "fsdp",
        scatter_dimension=0,
        tiled=True,
    ).astype(jnp.float32)
    grad_share, hvp_share = (
        lax.psum_scatter(owned[:, :width], "dp", scatter_dimension=1, tiled=True),
        lax.psum_scatter(owned[:, width:], "dp", scatter_dimension=1, tiled=True),
    )
    share_width = grad_share.shape[1]
    probe_cols = lax.dynamic_slice_in_dim(
        probe, lax.axis_index("dp") * share_width, share_width, 1
    ).astype(jnp.float32)
    return step_outputs(momentum, curvature, probe_cols, grad_share, hvp_share)


def pairs_of(move):
    def flat(y, z, x, c):
        return ((y * 4 + z) * 2 + x) * 2 + c

    found = []
    for y in range(2):
        for z in range(4):
            for x in range(2):
                for c in range(2):
                    target = move(y, z, x, c)
                    if target is not None:
                        found.append((flat(y, z, x, c), flat(*target)))
    return found


def send(value, move, name="exchange"):
    with jax.named_scope(name):
        return lax.ppermute(value, AXES, pairs_of(move))


def after(value, *earlier):
    return lax.optimization_barrier((value, *earlier))[0]


class Order:
    def __init__(self, token):
        self.token = token

    def wait(self, *values):
        *values, self.token = lax.optimization_barrier((*values, self.token))
        return values if len(values) > 1 else values[0]

    def run(self, operation, *values):
        *values, self.token = lax.optimization_barrier((*values, self.token))
        return self.wait(operation(*values))


def to_core(y, z, x, c):
    return (y, z, x, 1 - c)


def to_x(y, z, x, c):
    return (y, z, 1 - x, c)


def to_y(y, z, x, c):
    return (1 - y, z, x, c)


def to_first(y, z, x, c):
    return to_x(y, z, x, c) if c == 0 else to_y(y, z, x, c)


def to_second(y, z, x, c):
    return to_y(y, z, x, c) if c == 0 else to_x(y, z, x, c)


def to_corner(y, z, x, c):
    return to_x(y, z, x, c) if c == 0 else to_y(y, z, x, c)


def to_z(steps):
    return lambda y, z, x, c: (y, steps[z], x, c) if z in steps else None


Z_ONE = to_z({0: 1, 1: 0, 2: 3, 3: 2})
Z_IN = to_z({0: 1, 3: 2})
Z_MIDDLE = to_z({1: 2, 2: 1})
Z_OUT = to_z({1: 0, 2: 3})


VMEM = pl.BlockSpec(memory_space=pltpu.VMEM)
SMEM = pl.BlockSpec(memory_space=pltpu.SMEM)


def call(kernel, outs, scalars, *operands, name, cost=10**7):
    return pl.pallas_call(
        kernel,
        out_shape=outs,
        in_specs=[SMEM] + [VMEM] * len(operands),
        out_specs=jax.tree.map(lambda _: VMEM, outs),
        cost_estimate=pl.CostEstimate(flops=100 * cost, bytes_accessed=cost, transcendentals=0),
        compiler_params=pltpu.CompilerParams(vmem_limit_bytes=24 * 2**20),
        name=name,
    )(jnp.stack(scalars).astype(jnp.int32), *operands)


def dot(left, right):
    return jnp.dot(left, right, preferred_element_type=jnp.float32)


def halves(tokens):
    half = tokens.shape[0] // 2
    return pl.ds(0, half), pl.ds(half, half)


def partials(block, x, core, rights, tokens_ref, leave, out_ref):
    width = rights[0].shape[0] // 2
    depth = out_ref.shape[2]
    here, there = pl.ds(0, width), pl.ds(width, width)
    by_core = core == 0 if leave else core != 0
    place_fixed, place_by_core = 1 - x if leave else x, jnp.where(by_core, x, 1 - x)
    fixed = [right[there if leave else here, :] for right in rights]
    chosen = [jnp.where(by_core, right[there, :], right[here, :]) for right in rights]
    order = (0, 1) if leave else (1, 0)
    for i, place, lefts in ((order[0], place_fixed, fixed), (order[1], place_by_core, chosen)):
        for begin in range(0, depth, 256):
            size = min(256, depth - begin)
            at = pl.ds(pl.multiple_of((2 * block + place) * depth, 128) + begin, size)
            total = sum(
                dot(left, tokens_ref[rows, at]) for left, rows in zip(lefts, halves(tokens_ref))
            )
            out_ref[i, :, pl.ds(begin, size)] = total.astype(out_ref.dtype)


def contract(scalars, depth, leave, tokens, right_a, right_b):
    def kernel(at_ref, tokens_ref, right_a, right_b, out_ref):
        place = at_ref[0], at_ref[1], at_ref[2]
        partials(*place, (right_a, right_b), tokens_ref, leave, out_ref)

    dtype = jnp.bfloat16 if leave else jnp.float32
    out = jax.ShapeDtypeStruct((2, right_a.shape[0] // 2, depth), dtype)
    return call(kernel, out, scalars, tokens, right_a, right_b, name="contract", cost=10**7)


def head_gradients(scalars, depth, tokens, sums, own_up, other_up, norm_gain):
    half = tokens.shape[0] // 2
    width = sums[0].shape[1]
    head = norm_gain.shape[0]

    def kernel(
        at_ref, tokens_ref, own_ref, both_ref, first_ref, second_ref, up_a, up_b, gain_ref,
        right_a, right_b, leaving_ref,
    ):
        gain = gain_ref[...]
        own_first = at_ref[2] == 0
        for part, (up, right) in enumerate(((up_a, right_a), (up_b, right_b))):
            for begin in range(0, half, 128):
                size = min(128, half - begin)
                within = pl.ds(begin, size)
                at = pl.ds(part * half + begin, size)
                weighted = up[within, :].astype(jnp.float32)
                first, second = first_ref[at, :], second_ref[at, :]
                here = own_ref[at, :] + jnp.where(own_first, first, second)
                there = both_ref[at, :] + jnp.where(own_first, second, first)
                for side, product in enumerate((here, there)):
                    pair = head_terms(
                        product[:, :head],
                        product[:, head:],
                        weighted[:, side * head : (side + 1) * head] * gain,
                    )
                    for i, value in enumerate(pair):
                        features = pl.ds((2 * side + i) * head, head)
                        right[features, within] = value.T.astype(jnp.bfloat16)
        place = at_ref[0], at_ref[1], at_ref[2]
        partials(*place, (right_a, right_b), tokens_ref, True, leaving_ref)

    right = jax.ShapeDtypeStruct((2 * width, half), jnp.bfloat16)
    return call(
        kernel,
        [right, right, jax.ShapeDtypeStruct((2, width, depth), jnp.bfloat16)],
        scalars,
        tokens,
        *sums,
        own_up,
        other_up,
        norm_gain.reshape(1, head),
        name="head_gradients",
    )


def by_rows(scalars, *terms):
    width, depth = terms[0].shape
    half = depth // 2

    def kernel(at_ref, *refs):
        *term_refs, kept_ref, given_ref = refs

        def put(part, begin, value):
            rows = pl.ds(begin, value.shape[0])

            @pl.when(at_ref[2] == part)
            def _():
                kept_ref[rows, :] = value

            @pl.when(at_ref[2] != part)
            def _():
                given_ref[rows, :] = value

        for begin in range(0, depth, 128):
            size = min(128, depth - begin)
            total = sum(ref[:, pl.ds(begin, size)].astype(jnp.float32) for ref in term_refs).T
            below = max(0, min(size, half - begin))
            if below:
                put(0, begin, total[:below])
            if below < size:
                put(1, begin + below - half, total[below:])

    out = jax.ShapeDtypeStruct((half, width), jnp.float32)
    return call(kernel, [out, out], scalars, *terms, name="by_rows")


def finish(scalars, kept, taken, probe, momentum, curvature):
    head = kept.shape[1] // 2
    shares = momentum.shape[1] // head

    def kernel(at_ref, kept_ref, taken_ref, probe_ref, momentum_ref, curvature_ref, *out_refs):
        own_first = at_ref[0] == 0
        for i in range(shares):
            columns = pl.ds(i * head, head)
            mine = own_first if i == 0 else jnp.logical_not(own_first)
            share = jnp.where(mine, kept_ref[...], taken_ref[...])
            at = pl.multiple_of(at_ref[1] * (shares * head), 128) + i * head
            results = step_outputs(
                momentum_ref[:, columns],
                curvature_ref[:, columns],
                probe_ref[:, pl.ds(at, head)].astype(jnp.float32),
                share[:, :head],
                share[:, head:],
            )
            for out_ref, value in zip(out_refs, results):
                out_ref[:, columns] = value

    out = jax.ShapeDtypeStruct(momentum.shape, jnp.float32)
    return call(kernel, [out] * 3, scalars, kept, taken, probe, momentum, curvature, name="finish")


def columns_by_core(scalars, head, *arrays):
    rows = arrays[0].shape[0]

    def kernel(at_ref, *refs):
        *array_refs, leaving_ref, staying_ref = refs
        y, c = at_ref[0], at_ref[1]
        for out_ref, core in ((leaving_ref, 1 - c), (staying_ref, c)):
            for i, side in enumerate((y, 1 - y)):
                for j, ref in enumerate(array_refs):
                    column = pl.ds(pl.multiple_of((2 * side + core) * head, 128), head)
                    out_ref[:, pl.ds((i * len(array_refs) + j) * head, head)] = ref[:, column]

    out = jax.ShapeDtypeStruct((rows, 2 * len(arrays) * head), arrays[0].dtype)
    return call(kernel, [out, out], scalars, *arrays, name="columns_by_core")


def by_links(acts, upstream, k_weight, probe, norm_gain, momentum, curvature):
    head = norm_gain.shape[0]
    rows = k_weight.shape[0]
    place = lax.axis_index("fsdp")
    y, z, x, c = lax.axis_index("dp"), place // 4, (place // 2) % 2, place % 2
    own_first = c == 0

    leaving, staying = columns_by_core((y, c), head, k_weight, probe)
    coming = send(leaving, to_core, "coming")
    up_leaving, own_up = columns_by_core((y, c), head, after(upstream, leaving))
    other_up = send(up_leaving, to_core, "other_up")
    chip_rows = jnp.where(
        own_first,
        jnp.concatenate([staying, coming], axis=0),
        jnp.concatenate([coming, staying], axis=0),
    )
    mine, beside = chip_rows[:, : 2 * head], chip_rows[:, 2 * head :]

    order = Order(momentum)
    other_acts = send(after(acts, chip_rows), to_core, "other_acts")
    one = send(mine, Z_ONE, "one")
    near = send(mine, Z_MIDDLE, "near")
    across = send(mine, to_x, "across")
    other_up = order.wait(other_up)
    one, near = order.wait(one, near)
    two_out = send(near, Z_OUT, "two_out")
    two_in = send(one, Z_MIDDLE, "two_in")
    other_acts, one = order.wait(other_acts, one)
    one_first = send(one, to_first, "one_first")
    one_second = send(one, to_second, "one_second")
    corner = order.run(lambda a, b: jnp.where(own_first, a, b), beside, across)
    corner = send(corner, to_corner, "corner")
    tokens = order.run(lambda a, b: jnp.concatenate([a, b], axis=0), acts, other_acts)

    def block_of(held, slot, flip_x):
        start = ((z ^ slot) * 2 + (x ^ flip_x)) * (2 * rows)
        return lax.dynamic_slice_in_dim(held, start, 2 * rows, 1)

    def add_product(total, slot, flip_x, unit):
        def product(unit, held, *before):
            found = jnp.dot(block_of(held, slot, flip_x), unit, preferred_element_type=jnp.float32)
            return sum(before, found)

        return order.run(product, unit, tokens, *(() if total is None else (total,)))

    own_sum = add_product(None, 0, 0, mine)
    both_sum = add_product(None, 0, 0, beside)
    own_sum = add_product(own_sum, 0, 1, across)
    two_out, two_in = order.wait(two_out, two_in)
    two = order.run(jnp.add, two_out, two_in)
    three_out = send(two, Z_OUT, "three_out")
    two_first = send(two, to_first, "two_first")
    own_sum = add_product(own_sum, 1, 0, one)
    one_first = order.wait(one_first)
    one_both = send(one_first, to_second, "one_both")
    corner, two = order.wait(corner, two)
    two_second = send(two, to_second, "two_second")
    both_sum = add_product(both_sum, 0, 1, corner)
    first_sum = add_product(None, 1, 1 - c, one_first)
    second_sum = add_product(None, 1, c, one_second)
    own_sum = add_product(own_sum, 2, 0, two)
    three = order.run(jnp.add, near, three_out)
    three_first = send(three, to_first, "three_first")
    three_second = send(three, to_second, "three_second")
    both_sum = add_product(both_sum, 1, 1, one_both)
    two_first = order.wait(two_first)
    two_both = send(two_first, to_second, "two_both")
    first_sum = add_product(first_sum, 2, 1 - c, two_first)
    own_sum = add_product(own_sum, 3, 0, three)
    second_sum = add_product(second_sum, 2, c, two_second)
    three_first = order.wait(three_first)
    three_both = send(three_first, to_second, "three_both")
    first_sum = add_product(first_sum, 3, 1 - c, three_first)
    both_sum = add_product(both_sum, 2, 1, two_both)
    second_sum = add_product(second_sum, 3, c, three_second)
    both_sum = add_product(both_sum, 3, 1, three_both)

    sums = (own_sum, both_sum, first_sum, second_sum)
    right_a, right_b, leaving_3 = head_gradients(
        (z ^ 3, x, c), 2 * rows, tokens, sums, own_up, other_up, norm_gain
    )

    def partial(slot, leave):
        def product(*operands):
            return contract((z ^ slot, x, c), 2 * rows, leave, *operands)

        return order.run(product, tokens, right_a, right_b)

    def total_of(*terms):
        return sum((t.astype(jnp.float32) for t in terms[1:]), terms[0].astype(jnp.float32))

    def rounded(part, kept, got, *more):
        def total(kept, got, *more):
            return total_of(kept[part], got[part], *more).astype(jnp.bfloat16)

        return order.run(total, kept, got, *more)

    def sum_of(*terms):
        return order.run(lambda *t: total_of(*t).astype(jnp.bfloat16), *terms)

    seconds_3 = send(leaving_3, to_second, "seconds_3")
    raw_1 = send(partial(1, True), Z_ONE, "raw_1")
    seconds_2 = send(partial(2, True), to_second, "seconds_2")
    kept_3 = partial(3, False)
    first_3 = send(rounded(0, kept_3, seconds_3), to_first, "first_3")
    leaving_0 = partial(0, True)
    kept_2 = partial(2, False)
    kept_1 = partial(1, False)
    kept_0 = partial(0, False)
    leaving_0 = sum_of(leaving_0, raw_1)
    sum_3 = rounded(1, kept_3, seconds_3, first_3)
    three_in = send(sum_3, Z_IN, "three_in")
    first_2 = send(rounded(0, kept_2, seconds_2), to_first, "first_2")
    leaving_0 = order.wait(leaving_0)
    seconds_0 = send(leaving_0, to_second, "seconds_0")
    sum_2 = rounded(1, kept_2, seconds_2, first_2, three_in)
    two_in = send(sum_2, Z_IN, "two_in")
    two = send(sum_2, Z_MIDDLE, "two")
    first_1 = send(order.run(lambda kept: kept[0].astype(jnp.bfloat16), kept_1), to_first, "first_1")
    own_1 = order.run(lambda kept, got: total_of(kept[1], got), kept_1, first_1)
    first_0 = send(rounded(0, kept_0, seconds_0), to_first, "first_0")
    three = send(sum_of(sum_3, two_in), Z_MIDDLE, "three")
    one = send(sum_of(own_1, two), Z_ONE, "one")
    own_0 = order.run(lambda kept, got: total_of(kept[1], got[1]), kept_0, seconds_0)

    def turned(*terms):
        return by_rows((y, x, c), *terms)

    kept, given = order.run(turned, own_0, first_0, three, one)
    taken = send(given, to_core, "taken")
    return tuple(finish((c, y), kept, taken, probe, order.token, curvature))


def solution(mesh):
    on_links = mesh.shape["dp"] == 2 and mesh.shape["fsdp"] == 16
    return jax.shard_map(
        by_links if on_links else by_collectives,
        mesh=mesh,
        in_specs=(
            P(("dp", "fsdp"), None),
            P(("dp", "fsdp"), None),
            P("fsdp", None),
            P("fsdp", None),
            P(),
            P("fsdp", "dp"),
            P("fsdp", "dp"),
        ),
        out_specs=(P("fsdp", "dp"), P("fsdp", "dp"), P("fsdp", "dp")),
        check_vma=False,
    )
```

```python
import functools

import jax
import jax.numpy as jnp
from jax import lax
from jax.experimental import pallas as pl
from jax.experimental.pallas import tpu as pltpu
from jax.sharding import PartitionSpec as P

AXES = ("dp", "fsdp")


def contract_tokens(left, right):
    return lax.dot_general(
        left, right, (((0,), (0,)), ((), ())), preferred_element_type=jnp.float32
    )


def head_terms(values, moving, weighted):
    head_size = values.shape[-1]
    inverse = lax.rsqrt(jnp.mean(values * values, axis=-1, keepdims=True) + 1e-06)
    cubed = inverse * inverse * inverse
    along = jnp.sum(weighted * values, axis=-1, keepdims=True)
    grad_vals = inverse * weighted - cubed * values * along / head_size
    inverse_dot = -cubed * jnp.sum(values * moving, axis=-1, keepdims=True) / head_size
    along_dot = jnp.sum(weighted * moving, axis=-1, keepdims=True)
    hvp_vals = (
        inverse_dot * weighted
        - (
            3.0 * inverse * inverse * inverse_dot * values * along
            + cubed * moving * along
            + cubed * values * along_dot
        )
        / head_size
    )
    return grad_vals, hvp_vals


def step_outputs(momentum, curvature, probe_cols, grad_share, hvp_share):
    new_momentum = 0.965 * momentum + 0.035 * grad_share
    new_curvature = 0.99 * curvature + 0.01 * (probe_cols * hvp_share)
    update = jnp.clip(new_momentum / jnp.maximum(0.5 * new_curvature, 0.25), -1.0, 1.0)
    return (new_momentum, new_curvature, update)


def by_collectives(acts, upstream, k_weight, probe, norm_gain, momentum, curvature):
    width = k_weight.shape[1]
    weight_piece = lax.all_gather(k_weight, "fsdp", axis=0, tiled=True)
    probe_piece = lax.all_gather(probe, "fsdp", axis=0, tiled=True)
    projected = jnp.dot(acts, weight_piece, preferred_element_type=jnp.float32)
    tangent = jnp.dot(acts, probe_piece, preferred_element_type=jnp.float32)
    shaped = (acts.shape[0], -1, norm_gain.shape[0])
    weighted = upstream.astype(jnp.float32).reshape(shaped) * norm_gain
    pair = head_terms(projected.reshape(shaped), tangent.reshape(shaped), weighted)
    stacked = jnp.concatenate([v.reshape(acts.shape[0], -1) for v in pair], axis=1)
    owned = lax.psum_scatter(
        contract_tokens(acts, stacked.astype(jnp.bfloat16)).astype(jnp.bfloat16),
        "fsdp",
        scatter_dimension=0,
        tiled=True,
    ).astype(jnp.float32)
    grad_share, hvp_share = (
        lax.psum_scatter(owned[:, :width], "dp", scatter_dimension=1, tiled=True),
        lax.psum_scatter(owned[:, width:], "dp", scatter_dimension=1, tiled=True),
    )
    share_width = grad_share.shape[1]
    probe_cols = lax.dynamic_slice_in_dim(
        probe, lax.axis_index("dp") * share_width, share_width, 1
    ).astype(jnp.float32)
    return step_outputs(momentum, curvature, probe_cols, grad_share, hvp_share)


def pairs_of(move):
    def flat(y, z, x, c):
        return ((y * 4 + z) * 2 + x) * 2 + c

    found = []
    for y in range(2):
        for z in range(4):
            for x in range(2):
                for c in range(2):
                    target = move(y, z, x, c)
                    if target is not None:
                        found.append((flat(y, z, x, c), flat(*target)))
    return found


def send(value, move, name="exchange"):
    with jax.named_scope(name):
        return lax.ppermute(value, AXES, pairs_of(move))


def after(value, *earlier):
    return lax.optimization_barrier((value, *earlier))[0]


class Order:
    def __init__(self, token):
        self.token = token

    def wait(self, *values):
        *values, self.token = lax.optimization_barrier((*values, self.token))
        return values if len(values) > 1 else values[0]

    def run(self, operation, *values):
        *values, self.token = lax.optimization_barrier((*values, self.token))
        return self.wait(operation(*values))


def to_core(y, z, x, c):
    return (y, z, x, 1 - c)


def to_x(y, z, x, c):
    return (y, z, 1 - x, c)


def to_y(y, z, x, c):
    return (1 - y, z, x, c)


def to_first(y, z, x, c):
    return to_x(y, z, x, c) if c == 0 else to_y(y, z, x, c)


def to_second(y, z, x, c):
    return to_y(y, z, x, c) if c == 0 else to_x(y, z, x, c)


def to_corner(y, z, x, c):
    return to_x(y, z, x, c) if c == 0 else to_y(y, z, x, c)


def to_z(steps):
    return lambda y, z, x, c: (y, steps[z], x, c) if z in steps else None


Z_ONE = to_z({0: 1, 1: 0, 2: 3, 3: 2})
Z_IN = to_z({0: 1, 3: 2})
Z_MIDDLE = to_z({1: 2, 2: 1})
Z_OUT = to_z({1: 0, 2: 3})


VMEM = pl.BlockSpec(memory_space=pltpu.VMEM)
SMEM = pl.BlockSpec(memory_space=pltpu.SMEM)


def call(kernel, outs, scalars, *operands, name, cost=10**7, aliases=None):
    return pl.pallas_call(
        kernel,
        out_shape=outs,
        in_specs=[SMEM] + [VMEM] * len(operands),
        out_specs=jax.tree.map(lambda _: VMEM, outs),
        input_output_aliases=aliases or {},
        cost_estimate=pl.CostEstimate(flops=100 * cost, bytes_accessed=cost, transcendentals=0),
        compiler_params=pltpu.CompilerParams(vmem_limit_bytes=24 * 2**20),
        name=name,
    )(jnp.stack(scalars).astype(jnp.int32), *operands)


def dot(left, right):
    return jnp.dot(left, right, preferred_element_type=jnp.float32)


def halves(tokens):
    half = tokens.shape[0] // 2
    return pl.ds(0, half), pl.ds(half, half)


def partials(block, x, core, rights, tokens_ref, leave, out_ref):
    width = rights[0].shape[0] // 2
    depth = out_ref.shape[2]
    here, there = pl.ds(0, width), pl.ds(width, width)
    by_core = core == 0 if leave else core != 0
    place_fixed, place_by_core = 1 - x if leave else x, jnp.where(by_core, x, 1 - x)
    fixed = [right[there if leave else here, :] for right in rights]
    chosen = [jnp.where(by_core, right[there, :], right[here, :]) for right in rights]
    order = (0, 1) if leave else (1, 0)
    for i, place, lefts in ((order[0], place_fixed, fixed), (order[1], place_by_core, chosen)):
        for begin in range(0, depth, 256):
            size = min(256, depth - begin)
            at = pl.ds(pl.multiple_of((2 * block + place) * depth, 128) + begin, size)
            total = sum(
                dot(left, tokens_ref[rows, at]) for left, rows in zip(lefts, halves(tokens_ref))
            )
            out_ref[i, :, pl.ds(begin, size)] = total.astype(out_ref.dtype)


def contract(scalars, depth, leave, tokens, right_a, right_b):
    def kernel(at_ref, tokens_ref, right_a, right_b, out_ref):
        place = at_ref[0], at_ref[1], at_ref[2]
        partials(*place, (right_a, right_b), tokens_ref, leave, out_ref)

    dtype = jnp.bfloat16 if leave else jnp.float32
    out = jax.ShapeDtypeStruct((2, right_a.shape[0] // 2, depth), dtype)
    return call(kernel, out, scalars, tokens, right_a, right_b, name="contract", cost=10**7)


def head_gradients(scalars, depth, tokens, sums, own_up, other_up, norm_gain):
    half = tokens.shape[0] // 2
    width = sums[0].shape[1]
    head = norm_gain.shape[0]

    def kernel(
        at_ref, tokens_ref, own_ref, both_ref, first_ref, second_ref, up_a, up_b, gain_ref,
        right_a, right_b, leaving_ref,
    ):
        gain = gain_ref[...]
        own_first = at_ref[2] == 0
        for part, (up, right) in enumerate(((up_a, right_a), (up_b, right_b))):
            for begin in range(0, half, 128):
                size = min(128, half - begin)
                within = pl.ds(begin, size)
                at = pl.ds(part * half + begin, size)
                weighted = up[within, :].astype(jnp.float32)
                first, second = first_ref[at, :], second_ref[at, :]
                here = own_ref[at, :] + jnp.where(own_first, first, second)
                there = both_ref[at, :] + jnp.where(own_first, second, first)
                for side, product in enumerate((here, there)):
                    pair = head_terms(
                        product[:, :head],
                        product[:, head:],
                        weighted[:, side * head : (side + 1) * head] * gain,
                    )
                    for i, value in enumerate(pair):
                        features = pl.ds((2 * side + i) * head, head)
                        right[features, within] = value.T.astype(jnp.bfloat16)
        place = at_ref[0], at_ref[1], at_ref[2]
        partials(*place, (right_a, right_b), tokens_ref, True, leaving_ref)

    right = jax.ShapeDtypeStruct((2 * width, half), jnp.bfloat16)
    return call(
        kernel,
        [right, right, jax.ShapeDtypeStruct((2, width, depth), jnp.bfloat16)],
        scalars,
        tokens,
        *sums,
        own_up,
        other_up,
        norm_gain.reshape(1, head),
        name="head_gradients",
    )


def by_rows(scalars, *terms):
    width, depth = terms[0].shape
    half = depth // 2

    def kernel(at_ref, *refs):
        *term_refs, kept_ref, given_ref = refs

        def put(part, begin, value):
            rows = pl.ds(begin, value.shape[0])

            @pl.when(at_ref[2] == part)
            def _():
                kept_ref[rows, :] = value

            @pl.when(at_ref[2] != part)
            def _():
                given_ref[rows, :] = value

        for begin in range(0, depth, 128):
            size = min(128, depth - begin)
            total = sum(ref[:, pl.ds(begin, size)].astype(jnp.float32) for ref in term_refs).T
            below = max(0, min(size, half - begin))
            if below:
                put(0, begin, total[:below])
            if below < size:
                put(1, begin + below - half, total[below:])

    out = jax.ShapeDtypeStruct((half, width), jnp.float32)
    return call(kernel, [out, out], scalars, *terms, name="by_rows")


def finish(scalars, kept, taken, probe, momentum, curvature):
    head = kept.shape[1] // 2
    shares = momentum.shape[1] // head

    def kernel(at_ref, kept_ref, taken_ref, probe_ref, momentum_ref, curvature_ref, *out_refs):
        own_first = at_ref[0] == 0
        for i in range(shares):
            columns = pl.ds(i * head, head)
            mine = own_first if i == 0 else jnp.logical_not(own_first)
            share = jnp.where(mine, kept_ref[...], taken_ref[...])
            at = pl.multiple_of(at_ref[1] * (shares * head), 128) + i * head
            results = step_outputs(
                momentum_ref[:, columns],
                curvature_ref[:, columns],
                probe_ref[:, pl.ds(at, head)].astype(jnp.float32),
                share[:, :head],
                share[:, head:],
            )
            for out_ref, value in zip(out_refs, results):
                out_ref[:, columns] = value

    out = jax.ShapeDtypeStruct(momentum.shape, jnp.float32)
    return call(kernel, [out] * 3, scalars, kept, taken, probe, momentum, curvature, name="finish")


def unit_rows(scalars, head, weight, probe, units=()):
    rows = weight.shape[0]

    def kernel(at_ref, weight_ref, probe_ref, *refs):
        y, c = at_ref[0], at_ref[1]
        place = pl.ds(pl.multiple_of(at_ref[2] * rows, 16), rows)
        for side, out_ref in zip((y, 1 - y), refs[-2:]):
            column = pl.ds(pl.multiple_of((2 * side + c) * head, 128), head)
            for j, ref in enumerate((weight_ref, probe_ref)):
                out_ref[place, pl.ds(j * head, head)] = ref[:, column]

    out = jax.ShapeDtypeStruct((2 * rows, 2 * head), weight.dtype)
    aliases = {3: 0, 4: 1} if units else {}
    return call(kernel, [out, out], scalars, weight, probe, *units, name="unit_rows", aliases=aliases)


def columns_by_core(scalars, head, *arrays):
    rows = arrays[0].shape[0]

    def kernel(at_ref, *refs):
        *array_refs, leaving_ref, staying_ref = refs
        y, c = at_ref[0], at_ref[1]
        for out_ref, core in ((leaving_ref, 1 - c), (staying_ref, c)):
            for i, side in enumerate((y, 1 - y)):
                for j, ref in enumerate(array_refs):
                    column = pl.ds(pl.multiple_of((2 * side + core) * head, 128), head)
                    out_ref[:, pl.ds((i * len(array_refs) + j) * head, head)] = ref[:, column]

    out = jax.ShapeDtypeStruct((rows, 2 * len(arrays) * head), arrays[0].dtype)
    return call(kernel, [out, out], scalars, *arrays, name="columns_by_core")


def by_links(acts, upstream, k_weight, probe, norm_gain, momentum, curvature):
    head = norm_gain.shape[0]
    rows = k_weight.shape[0]
    place = lax.axis_index("fsdp")
    y, z, x, c = lax.axis_index("dp"), place // 4, (place // 2) % 2, place % 2
    own_first = c == 0

    other_weight, other_probe = send(k_weight, to_core, "other_weight"), send(probe, to_core, "other_probe")
    own_rows = unit_rows((y, c, c), head, k_weight, probe)
    mine, beside = unit_rows((y, c, 1 - c), head, other_weight, other_probe, own_rows)
    up_leaving, own_up = columns_by_core((y, c), head, after(upstream, mine))
    other_up = send(up_leaving, to_core, "other_up")
    order = Order(momentum)
    other_acts = send(after(acts, mine), to_core, "other_acts")
    one = send(mine, Z_ONE, "one")
    near = send(mine, Z_MIDDLE, "near")
    across = send(mine, to_x, "across")
    other_up = order.wait(other_up)
    one, near = order.wait(one, near)
    two_out = send(near, Z_OUT, "two_out")
    two_in = send(one, Z_MIDDLE, "two_in")
    other_acts, one = order.wait(other_acts, one)
    one_first = send(one, to_first, "one_first")
    corner = order.run(lambda a, b: jnp.where(own_first, a, b), beside, across)
    corner = send(corner, to_corner, "corner")
    tokens = order.run(lambda a, b: jnp.concatenate([a, b], axis=0), acts, other_acts)

    def block_of(held, slot, flip_x):
        start = ((z ^ slot) * 2 + (x ^ flip_x)) * (2 * rows)
        return lax.dynamic_slice_in_dim(held, start, 2 * rows, 1)

    def add_product(total, slot, flip_x, unit):
        def product(unit, held, *before):
            found = jnp.dot(block_of(held, slot, flip_x), unit, preferred_element_type=jnp.float32)
            return sum(before, found)

        return order.run(product, unit, tokens, *(() if total is None else (total,)))

    own_sum = add_product(None, 0, 0, mine)
    both_sum = add_product(None, 0, 0, beside)
    own_sum = add_product(own_sum, 0, 1, across)
    two_out, two_in = order.wait(two_out, two_in)
    two = order.run(jnp.add, two_out, two_in)
    three_out = send(two, Z_OUT, "three_out")
    two_first = send(two, to_first, "two_first")
    own_sum = add_product(own_sum, 1, 0, one)
    one_first = order.wait(one_first)
    one_both = send(one_first, to_second, "one_both")
    corner, two = order.wait(corner, two)
    two_second = send(two, to_second, "two_second")
    both_sum = add_product(both_sum, 0, 1, corner)
    first_sum = add_product(None, 1, 1 - c, one_first)
    own_sum = add_product(own_sum, 2, 0, two)
    three = order.run(jnp.add, near, three_out)
    three_first = send(three, to_first, "three_first")
    flip = order.run(lambda a, b: jnp.where(own_first, a, b), beside, across)
    one_second = send(flip, Z_ONE, "one_second")
    three_second = send(three, to_second, "three_second")
    both_sum = add_product(both_sum, 1, 1, one_both)
    two_first = order.wait(two_first)
    two_both = send(two_first, to_second, "two_both")
    first_sum = add_product(first_sum, 2, 1 - c, two_first)
    own_sum = add_product(own_sum, 3, 0, three)
    second_sum = add_product(None, 2, c, two_second)
    three_first = order.wait(three_first)
    three_both = send(three_first, to_second, "three_both")
    first_sum = add_product(first_sum, 3, 1 - c, three_first)
    both_sum = add_product(both_sum, 2, 1, two_both)
    second_sum = add_product(second_sum, 1, c, one_second)
    second_sum = add_product(second_sum, 3, c, three_second)
    both_sum = add_product(both_sum, 3, 1, three_both)

    sums = (own_sum, both_sum, first_sum, second_sum)
    right_a, right_b, leaving_3 = head_gradients(
        (z ^ 3, x, c), 2 * rows, tokens, sums, own_up, other_up, norm_gain
    )

    def partial(slot, leave):
        def product(*operands):
            return contract((z ^ slot, x, c), 2 * rows, leave, *operands)

        return order.run(product, tokens, right_a, right_b)

    def total_of(*terms):
        return sum((t.astype(jnp.float32) for t in terms[1:]), terms[0].astype(jnp.float32))

    def rounded(part, kept, got, *more):
        def total(kept, got, *more):
            return total_of(kept[part], got[part], *more).astype(jnp.bfloat16)

        return order.run(total, kept, got, *more)

    def sum_of(*terms):
        return order.run(lambda *t: total_of(*t).astype(jnp.bfloat16), *terms)

    seconds_3 = send(leaving_3, to_second, "seconds_3")
    raw_1 = send(partial(1, True), Z_ONE, "raw_1")
    seconds_2 = send(partial(2, True), to_second, "seconds_2")
    kept_3 = partial(3, False)
    first_3 = send(rounded(0, kept_3, seconds_3), to_first, "first_3")
    leaving_0 = partial(0, True)
    kept_2 = partial(2, False)
    kept_1 = partial(1, False)
    kept_0 = partial(0, False)
    leaving_0 = sum_of(leaving_0, raw_1)
    sum_3 = rounded(1, kept_3, seconds_3, first_3)
    three_in = send(sum_3, Z_IN, "three_in")
    first_2 = send(rounded(0, kept_2, seconds_2), to_first, "first_2")
    first_1 = send(order.run(lambda kept: kept[0].astype(jnp.bfloat16), kept_1), to_first, "first_1")
    leaving_0 = order.wait(leaving_0)
    seconds_0 = send(leaving_0, to_second, "seconds_0")
    sum_2 = rounded(1, kept_2, seconds_2, first_2, three_in)
    two_in = send(sum_2, Z_IN, "two_in")
    two = send(sum_2, Z_MIDDLE, "two")
    own_1 = order.run(lambda kept, got: total_of(kept[1], got), kept_1, first_1)
    first_0 = send(rounded(0, kept_0, seconds_0), to_first, "first_0")
    three = send(sum_of(sum_3, two_in), Z_MIDDLE, "three")
    one = send(sum_of(own_1, two), Z_ONE, "one")
    own_0 = order.run(lambda kept, got: total_of(kept[1], got[1]), kept_0, seconds_0)

    def turned(*terms):
        return by_rows((y, x, c), *terms)

    kept, given = order.run(turned, own_0, first_0, three, one)
    taken = send(given, to_core, "taken")
    return tuple(finish((c, y), kept, taken, probe, order.token, curvature))


def solution(mesh):
    on_links = mesh.shape["dp"] == 2 and mesh.shape["fsdp"] == 16
    return jax.shard_map(
        by_links if on_links else by_collectives,
        mesh=mesh,
        in_specs=(
            P(("dp", "fsdp"), None),
            P(("dp", "fsdp"), None),
            P("fsdp", None),
            P("fsdp", None),
            P(),
            P("fsdp", "dp"),
            P("fsdp", "dp"),
        ),
        out_specs=(P("fsdp", "dp"), P("fsdp", "dp"), P("fsdp", "dp")),
        check_vma=False,
    )
```

```python
import functools

import jax
import jax.numpy as jnp
from jax import lax
from jax.experimental import pallas as pl
from jax.experimental.pallas import tpu as pltpu
from jax.sharding import PartitionSpec as P

AXES = ("dp", "fsdp")


def contract_tokens(left, right):
    return lax.dot_general(
        left, right, (((0,), (0,)), ((), ())), preferred_element_type=jnp.float32
    )


def head_terms(values, moving, weighted):
    head_size = values.shape[-1]
    inverse = lax.rsqrt(jnp.mean(values * values, axis=-1, keepdims=True) + 1e-06)
    cubed = inverse * inverse * inverse
    along = jnp.sum(weighted * values, axis=-1, keepdims=True)
    grad_vals = inverse * weighted - cubed * values * along / head_size
    inverse_dot = -cubed * jnp.sum(values * moving, axis=-1, keepdims=True) / head_size
    along_dot = jnp.sum(weighted * moving, axis=-1, keepdims=True)
    hvp_vals = (
        inverse_dot * weighted
        - (
            3.0 * inverse * inverse * inverse_dot * values * along
            + cubed * moving * along
            + cubed * values * along_dot
        )
        / head_size
    )
    return grad_vals, hvp_vals


def step_outputs(momentum, curvature, probe_cols, grad_share, hvp_share):
    new_momentum = 0.965 * momentum + 0.035 * grad_share
    new_curvature = 0.99 * curvature + 0.01 * (probe_cols * hvp_share)
    update = jnp.clip(new_momentum / jnp.maximum(0.5 * new_curvature, 0.25), -1.0, 1.0)
    return (new_momentum, new_curvature, update)


def by_collectives(acts, upstream, k_weight, probe, norm_gain, momentum, curvature):
    width = k_weight.shape[1]
    weight_piece = lax.all_gather(k_weight, "fsdp", axis=0, tiled=True)
    probe_piece = lax.all_gather(probe, "fsdp", axis=0, tiled=True)
    projected = jnp.dot(acts, weight_piece, preferred_element_type=jnp.float32)
    tangent = jnp.dot(acts, probe_piece, preferred_element_type=jnp.float32)
    shaped = (acts.shape[0], -1, norm_gain.shape[0])
    weighted = upstream.astype(jnp.float32).reshape(shaped) * norm_gain
    pair = head_terms(projected.reshape(shaped), tangent.reshape(shaped), weighted)
    stacked = jnp.concatenate([v.reshape(acts.shape[0], -1) for v in pair], axis=1)
    owned = lax.psum_scatter(
        contract_tokens(acts, stacked.astype(jnp.bfloat16)).astype(jnp.bfloat16),
        "fsdp",
        scatter_dimension=0,
        tiled=True,
    ).astype(jnp.float32)
    grad_share, hvp_share = (
        lax.psum_scatter(owned[:, :width], "dp", scatter_dimension=1, tiled=True),
        lax.psum_scatter(owned[:, width:], "dp", scatter_dimension=1, tiled=True),
    )
    share_width = grad_share.shape[1]
    probe_cols = lax.dynamic_slice_in_dim(
        probe, lax.axis_index("dp") * share_width, share_width, 1
    ).astype(jnp.float32)
    return step_outputs(momentum, curvature, probe_cols, grad_share, hvp_share)


def pairs_of(move):
    def flat(y, z, x, c):
        return ((y * 4 + z) * 2 + x) * 2 + c

    found = []
    for y in range(2):
        for z in range(4):
            for x in range(2):
                for c in range(2):
                    target = move(y, z, x, c)
                    if target is not None:
                        found.append((flat(y, z, x, c), flat(*target)))
    return found


def send(value, move, name="exchange"):
    with jax.named_scope(name):
        return lax.ppermute(value, AXES, pairs_of(move))


def after(value, *earlier):
    return lax.optimization_barrier((value, *earlier))[0]


class Order:
    def __init__(self, token):
        self.token = token

    def wait(self, *values):
        *values, self.token = lax.optimization_barrier((*values, self.token))
        return values if len(values) > 1 else values[0]

    def run(self, operation, *values):
        *values, self.token = lax.optimization_barrier((*values, self.token))
        found = operation(*values)
        return self.wait(*found) if isinstance(found, (list, tuple)) else self.wait(found)


def to_core(y, z, x, c):
    return (y, z, x, 1 - c)


def to_x(y, z, x, c):
    return (y, z, 1 - x, c)


def to_y(y, z, x, c):
    return (1 - y, z, x, c)


def to_first(y, z, x, c):
    return to_x(y, z, x, c) if c == 0 else to_y(y, z, x, c)


def to_second(y, z, x, c):
    return to_y(y, z, x, c) if c == 0 else to_x(y, z, x, c)


def to_corner(y, z, x, c):
    return to_x(y, z, x, c) if c == 0 else to_y(y, z, x, c)


def to_z(steps):
    return lambda y, z, x, c: (y, steps[z], x, c) if z in steps else None


Z_ONE = to_z({0: 1, 1: 0, 2: 3, 3: 2})
Z_IN = to_z({0: 1, 3: 2})
Z_MIDDLE = to_z({1: 2, 2: 1})
Z_OUT = to_z({1: 0, 2: 3})


VMEM = pl.BlockSpec(memory_space=pltpu.VMEM)
SMEM = pl.BlockSpec(memory_space=pltpu.SMEM)


def call(kernel, outs, scalars, *operands, name, cost=10**7, aliases=None):
    return pl.pallas_call(
        kernel,
        out_shape=outs,
        in_specs=[SMEM] + [VMEM] * len(operands),
        out_specs=jax.tree.map(lambda _: VMEM, outs),
        input_output_aliases=aliases or {},
        cost_estimate=pl.CostEstimate(flops=100 * cost, bytes_accessed=cost, transcendentals=0),
        compiler_params=pltpu.CompilerParams(vmem_limit_bytes=24 * 2**20),
        name=name,
    )(jnp.stack(scalars).astype(jnp.int32), *operands)


def dot(left, right):
    return jnp.dot(left, right, preferred_element_type=jnp.float32)


def halves(tokens):
    half = tokens.shape[0] // 2
    return pl.ds(0, half), pl.ds(half, half)


def partials(block, x, core, heres, theres, tokens_ref, leave, out_ref):
    depth = out_ref.shape[2]
    by_core = core == 0 if leave else core != 0
    place_fixed, place_by_core = 1 - x if leave else x, jnp.where(by_core, x, 1 - x)
    fixed = [ref[...] for ref in (theres if leave else heres)]
    chosen = [jnp.where(by_core, there[...], here[...]) for here, there in zip(heres, theres)]
    order = (0, 1) if leave else (1, 0)
    for i, place, lefts in ((order[0], place_fixed, fixed), (order[1], place_by_core, chosen)):
        for begin in range(0, depth, 256):
            size = min(256, depth - begin)
            at = pl.ds(pl.multiple_of((2 * block + place) * depth, 128) + begin, size)
            total = sum(
                dot(left, tokens_ref[rows, at]) for left, rows in zip(lefts, halves(tokens_ref))
            )
            out_ref[i, :, pl.ds(begin, size)] = total.astype(out_ref.dtype)


def contract(scalars, depth, leave, tokens, *rights):
    def kernel(at_ref, tokens_ref, here_a, here_b, there_a, there_b, out_ref):
        place = at_ref[0], at_ref[1], at_ref[2]
        partials(*place, (here_a, here_b), (there_a, there_b), tokens_ref, leave, out_ref)

    dtype = jnp.bfloat16 if leave else jnp.float32
    out = jax.ShapeDtypeStruct((2, rights[0].shape[0], depth), dtype)
    return call(kernel, out, scalars, tokens, *rights, name="contract")


def turned_gradients(product_of, up_refs, column, gain, out_refs):
    head = gain.shape[1]
    for part, (up_ref, out_ref) in enumerate(zip(up_refs, out_refs)):
        half = up_ref.shape[0]
        for begin in range(0, half, 128):
            size = min(128, half - begin)
            within = pl.ds(begin, size)
            product = product_of(part, begin, size)
            weighted = up_ref[within, column].astype(jnp.float32) * gain
            pair = head_terms(product[:, :head], product[:, head:], weighted)
            for i, value in enumerate(pair):
                out_ref[pl.ds(i * head, head), within] = value.T.astype(jnp.bfloat16)


def side_column(at_ref, side, head):
    return pl.ds(pl.multiple_of((2 * side + at_ref[2]) * head, 128), head)


def gradients_here(scalars, own, first, second, upstream, other_up, norm_gain):
    half, width = own.shape[0] // 2, own.shape[1]
    head = norm_gain.shape[0]

    def kernel(at_ref, own_ref, first_ref, second_ref, up_a, up_b, gain_ref, *out_refs):
        own_first = at_ref[2] == 0

        def product_of(part, begin, size):
            at = pl.ds(part * half + begin, size)
            return own_ref[at, :] + jnp.where(own_first, first_ref[at, :], second_ref[at, :])

        column = side_column(at_ref, at_ref[3], head)
        turned_gradients(product_of, (up_a, up_b), column, gain_ref[...], out_refs)

    out = jax.ShapeDtypeStruct((width, half), jnp.bfloat16)
    operands = (own, first, second, upstream, other_up, norm_gain.reshape(1, head))
    return call(kernel, [out, out], scalars, *operands, name="gradients_here")


def gradients_there(scalars, tokens, heres, both, first, second, last, upstream, other_up, norm_gain):
    half, width = both.shape[0] // 2, both.shape[1]
    depth = last.shape[0]
    head = norm_gain.shape[0]

    def kernel(
        at_ref, tokens_ref, here_a, here_b, both_ref, first_ref, second_ref, last_ref, up_a, up_b, gain_ref,
        there_a, there_b, leaving_ref,
    ):
        block, x, core = at_ref[0], at_ref[1], at_ref[2]
        far = pl.ds(pl.multiple_of((2 * block + 1 - x) * depth, 128), depth)
        products = [dot(tokens_ref[rows, far], last_ref[...]) for rows in halves(tokens)]

        def product_of(part, begin, size):
            at = pl.ds(part * half + begin, size)
            by_core = jnp.where(core == 0, second_ref[at, :], first_ref[at, :])
            return both_ref[at, :] + by_core + products[part][begin : begin + size]

        column = side_column(at_ref, 1 - at_ref[3], head)
        turned_gradients(product_of, (up_a, up_b), column, gain_ref[...], (there_a, there_b))
        partials(
            block, x, core, (here_a, here_b), (there_a, there_b), tokens_ref, True, leaving_ref
        )

    out = jax.ShapeDtypeStruct((width, half), jnp.bfloat16)
    leaving = jax.ShapeDtypeStruct((2, width, depth), jnp.bfloat16)
    operands = (*heres, both, first, second, last, upstream, other_up, norm_gain.reshape(1, head))
    return call(kernel, [out, out, leaving], scalars, tokens, *operands, name="gradients_there")


def by_rows(scalars, *terms):
    width, depth = terms[0].shape
    half = depth // 2

    def kernel(at_ref, *refs):
        *term_refs, kept_ref, given_ref = refs

        def put(part, begin, value):
            rows = pl.ds(begin, value.shape[0])

            @pl.when(at_ref[2] == part)
            def _():
                kept_ref[rows, :] = value

            @pl.when(at_ref[2] != part)
            def _():
                given_ref[rows, :] = value

        for begin in range(0, depth, 128):
            size = min(128, depth - begin)
            total = sum(ref[:, pl.ds(begin, size)].astype(jnp.float32) for ref in term_refs).T
            below = max(0, min(size, half - begin))
            if below:
                put(0, begin, total[:below])
            if below < size:
                put(1, begin + below - half, total[below:])

    out = jax.ShapeDtypeStruct((half, width), jnp.float32)
    return call(kernel, [out, out], scalars, *terms, name="by_rows")


def finish(scalars, kept, taken, probe, momentum, curvature):
    head = kept.shape[1] // 2
    shares = momentum.shape[1] // head

    def kernel(at_ref, kept_ref, taken_ref, probe_ref, momentum_ref, curvature_ref, *out_refs):
        own_first = at_ref[0] == 0
        for i in range(shares):
            columns = pl.ds(i * head, head)
            mine = own_first if i == 0 else jnp.logical_not(own_first)
            share = jnp.where(mine, kept_ref[...], taken_ref[...])
            at = pl.multiple_of(at_ref[1] * (shares * head), 128) + i * head
            results = step_outputs(
                momentum_ref[:, columns],
                curvature_ref[:, columns],
                probe_ref[:, pl.ds(at, head)].astype(jnp.float32),
                share[:, :head],
                share[:, head:],
            )
            for out_ref, value in zip(out_refs, results):
                out_ref[:, columns] = value

    out = jax.ShapeDtypeStruct(momentum.shape, jnp.float32)
    return call(kernel, [out] * 3, scalars, kept, taken, probe, momentum, curvature, name="finish")


def unit_rows(scalars, head, weight, probe, units=()):
    rows = weight.shape[0]

    def kernel(at_ref, weight_ref, probe_ref, *refs):
        y, c = at_ref[0], at_ref[1]
        place = pl.ds(pl.multiple_of(at_ref[2] * rows, 16), rows)
        for side, out_ref in zip((y, 1 - y), refs[-2:]):
            column = pl.ds(pl.multiple_of((2 * side + c) * head, 128), head)
            for j, ref in enumerate((weight_ref, probe_ref)):
                out_ref[place, pl.ds(j * head, head)] = ref[:, column]

    out = jax.ShapeDtypeStruct((2 * rows, 2 * head), weight.dtype)
    aliases = {3: 0, 4: 1} if units else {}
    return call(kernel, [out, out], scalars, weight, probe, *units, name="unit_rows", aliases=aliases)


def by_links(acts, upstream, k_weight, probe, norm_gain, momentum, curvature):
    head = norm_gain.shape[0]
    rows = k_weight.shape[0]
    place = lax.axis_index("fsdp")
    y, z, x, c = lax.axis_index("dp"), place // 4, (place // 2) % 2, place % 2
    own_first = c == 0

    other_weight, other_probe = send(k_weight, to_core, "other_weight"), send(probe, to_core, "other_probe")
    own_rows = unit_rows((y, c, c), head, k_weight, probe)
    mine, beside = unit_rows((y, c, 1 - c), head, other_weight, other_probe, own_rows)
    other_up = send(upstream, to_core, "other_up")
    order = Order(momentum)
    other_acts = send(after(acts, mine), to_core, "other_acts")
    one = send(mine, Z_ONE, "one")
    near = send(mine, Z_MIDDLE, "near")
    across = send(mine, to_x, "across")
    other_up = order.wait(other_up)
    one, near = order.wait(one, near)
    two_out = send(near, Z_OUT, "two_out")
    two_in = send(one, Z_MIDDLE, "two_in")
    other_acts, one = order.wait(other_acts, one)
    one_first = send(one, to_first, "one_first")
    corner = order.run(lambda a, b: jnp.where(own_first, a, b), beside, across)
    corner = send(corner, to_corner, "corner")
    tokens = order.run(lambda a, b: jnp.concatenate([a, b], axis=0), acts, other_acts)

    def block_of(held, slot, flip_x):
        start = ((z ^ slot) * 2 + (x ^ flip_x)) * (2 * rows)
        return lax.dynamic_slice_in_dim(held, start, 2 * rows, 1)

    def add_product(total, slot, flip_x, unit):
        def product(unit, held, *before):
            found = jnp.dot(block_of(held, slot, flip_x), unit, preferred_element_type=jnp.float32)
            return sum(before, found)

        return order.run(product, unit, tokens, *(() if total is None else (total,)))

    own_sum = add_product(None, 0, 0, mine)
    both_sum = add_product(None, 0, 0, beside)
    own_sum = add_product(own_sum, 0, 1, across)
    two_out, two_in = order.wait(two_out, two_in)
    two = order.run(jnp.add, two_out, two_in)
    three_out = send(two, Z_OUT, "three_out")
    own_sum = add_product(own_sum, 1, 0, one)
    one_first = order.wait(one_first)
    one_both = send(one_first, to_second, "one_both")
    corner, two = order.wait(corner, two)
    two_first = send(two, to_first, "two_first")
    two_second = send(two, to_second, "two_second")
    both_sum = add_product(both_sum, 0, 1, corner)
    first_sum = add_product(None, 1, 1 - c, one_first)
    own_sum = add_product(own_sum, 2, 0, two)
    three = order.run(jnp.add, near, three_out)
    three_first = send(three, to_first, "three_first")
    flip = order.run(lambda a, b: jnp.where(own_first, a, b), beside, across)
    one_second = send(flip, Z_ONE, "one_second")
    three_second = send(three, to_second, "three_second")
    two_first = order.wait(two_first)
    two_both = send(two_first, to_second, "two_both")
    both_sum = add_product(both_sum, 1, 1, one_both)
    first_sum = add_product(first_sum, 2, 1 - c, two_first)
    own_sum = add_product(own_sum, 3, 0, three)
    second_sum = add_product(None, 2, c, two_second)
    three_first = order.wait(three_first)
    three_both = send(three_first, to_second, "three_both")
    first_sum = add_product(first_sum, 3, 1 - c, three_first)
    both_sum = add_product(both_sum, 2, 1, two_both)
    second_sum = add_product(second_sum, 1, c, one_second)
    second_sum = add_product(second_sum, 3, c, three_second)
    place = (z ^ 3, x, c, y)
    ups = (upstream, other_up, norm_gain)
    heres = order.run(
        lambda *sums: gradients_here(place, *sums, *ups), own_sum, first_sum, second_sum
    )
    *theres, leaving_3 = gradients_there(
        place, tokens, heres, both_sum, first_sum, second_sum, order.wait(three_both), *ups
    )

    def partial(slot, leave):
        def product(*operands):
            return contract((z ^ slot, x, c), 2 * rows, leave, *operands)

        return order.run(product, tokens, *heres, *theres)

    def total_of(*terms):
        return sum((t.astype(jnp.float32) for t in terms[1:]), terms[0].astype(jnp.float32))

    def rounded(part, kept, got, *more):
        def total(kept, got, *more):
            return total_of(kept[part], got[part], *more).astype(jnp.bfloat16)

        return order.run(total, kept, got, *more)

    def sum_of(*terms):
        return order.run(lambda *t: total_of(*t).astype(jnp.bfloat16), *terms)

    seconds_3 = send(leaving_3, to_second, "seconds_3")
    raw_1 = send(partial(1, True), Z_ONE, "raw_1")
    seconds_2 = send(partial(2, True), to_second, "seconds_2")
    kept_3 = partial(3, False)
    first_3 = send(rounded(0, kept_3, seconds_3), to_first, "first_3")
    leaving_0 = partial(0, True)
    kept_2 = partial(2, False)
    kept_1 = partial(1, False)
    kept_0 = partial(0, False)
    leaving_0 = sum_of(leaving_0, raw_1)
    sum_3 = rounded(1, kept_3, seconds_3, first_3)
    three_in = send(sum_3, Z_IN, "three_in")
    first_2 = send(rounded(0, kept_2, seconds_2), to_first, "first_2")
    first_1 = send(order.run(lambda kept: kept[0].astype(jnp.bfloat16), kept_1), to_first, "first_1")
    leaving_0 = order.wait(leaving_0)
    seconds_0 = send(leaving_0, to_second, "seconds_0")
    sum_2 = rounded(1, kept_2, seconds_2, first_2, three_in)
    two_in = send(sum_2, Z_IN, "two_in")
    two = send(sum_2, Z_MIDDLE, "two")
    own_1 = order.run(lambda kept, got: total_of(kept[1], got), kept_1, first_1)
    first_0 = send(rounded(0, kept_0, seconds_0), to_first, "first_0")
    three = send(sum_of(sum_3, two_in), Z_MIDDLE, "three")
    one = send(sum_of(own_1, two), Z_ONE, "one")
    own_0 = order.run(lambda kept, got: total_of(kept[1], got[1]), kept_0, seconds_0)

    def turned(*terms):
        return by_rows((y, x, c), *terms)

    kept, given = order.run(turned, own_0, first_0, three, one)
    taken = send(given, to_core, "taken")
    return tuple(finish((c, y), kept, taken, probe, order.token, curvature))


def solution(mesh):
    on_links = mesh.shape["dp"] == 2 and mesh.shape["fsdp"] == 16
    return jax.shard_map(
        by_links if on_links else by_collectives,
        mesh=mesh,
        in_specs=(
            P(("dp", "fsdp"), None),
            P(("dp", "fsdp"), None),
            P("fsdp", None),
            P("fsdp", None),
            P(),
            P("fsdp", "dp"),
            P("fsdp", "dp"),
        ),
        out_specs=(P("fsdp", "dp"), P("fsdp", "dp"), P("fsdp", "dp")),
        check_vma=False,
    )
```

```python
import functools

import jax
import jax.numpy as jnp
from jax import lax
from jax.experimental import pallas as pl
from jax.experimental.pallas import tpu as pltpu
from jax.sharding import PartitionSpec as P

AXES = ("dp", "fsdp")


def contract_tokens(left, right):
    return lax.dot_general(
        left, right, (((0,), (0,)), ((), ())), preferred_element_type=jnp.float32
    )


def head_terms(values, moving, weighted):
    head_size = values.shape[-1]
    inverse = lax.rsqrt(jnp.mean(values * values, axis=-1, keepdims=True) + 1e-06)
    cubed = inverse * inverse * inverse
    along = jnp.sum(weighted * values, axis=-1, keepdims=True)
    grad_vals = inverse * weighted - cubed * values * along / head_size
    inverse_dot = -cubed * jnp.sum(values * moving, axis=-1, keepdims=True) / head_size
    along_dot = jnp.sum(weighted * moving, axis=-1, keepdims=True)
    hvp_vals = (
        inverse_dot * weighted
        - (
            3.0 * inverse * inverse * inverse_dot * values * along
            + cubed * moving * along
            + cubed * values * along_dot
        )
        / head_size
    )
    return grad_vals, hvp_vals


def step_outputs(momentum, curvature, probe_cols, grad_share, hvp_share):
    new_momentum = 0.965 * momentum + 0.035 * grad_share
    new_curvature = 0.99 * curvature + 0.01 * (probe_cols * hvp_share)
    update = jnp.clip(new_momentum / jnp.maximum(0.5 * new_curvature, 0.25), -1.0, 1.0)
    return (new_momentum, new_curvature, update)


def by_collectives(acts, upstream, k_weight, probe, norm_gain, momentum, curvature):
    width = k_weight.shape[1]
    weight_piece = lax.all_gather(k_weight, "fsdp", axis=0, tiled=True)
    probe_piece = lax.all_gather(probe, "fsdp", axis=0, tiled=True)
    projected = jnp.dot(acts, weight_piece, preferred_element_type=jnp.float32)
    tangent = jnp.dot(acts, probe_piece, preferred_element_type=jnp.float32)
    shaped = (acts.shape[0], -1, norm_gain.shape[0])
    weighted = upstream.astype(jnp.float32).reshape(shaped) * norm_gain
    pair = head_terms(projected.reshape(shaped), tangent.reshape(shaped), weighted)
    stacked = jnp.concatenate([v.reshape(acts.shape[0], -1) for v in pair], axis=1)
    owned = lax.psum_scatter(
        contract_tokens(acts, stacked.astype(jnp.bfloat16)).astype(jnp.bfloat16),
        "fsdp",
        scatter_dimension=0,
        tiled=True,
    ).astype(jnp.float32)
    grad_share, hvp_share = (
        lax.psum_scatter(owned[:, :width], "dp", scatter_dimension=1, tiled=True),
        lax.psum_scatter(owned[:, width:], "dp", scatter_dimension=1, tiled=True),
    )
    share_width = grad_share.shape[1]
    probe_cols = lax.dynamic_slice_in_dim(
        probe, lax.axis_index("dp") * share_width, share_width, 1
    ).astype(jnp.float32)
    return step_outputs(momentum, curvature, probe_cols, grad_share, hvp_share)


def pairs_of(move):
    def flat(y, z, x, c):
        return ((y * 4 + z) * 2 + x) * 2 + c

    found = []
    for y in range(2):
        for z in range(4):
            for x in range(2):
                for c in range(2):
                    target = move(y, z, x, c)
                    if target is not None:
                        found.append((flat(y, z, x, c), flat(*target)))
    return found


def send(value, move, name="exchange"):
    with jax.named_scope(name):
        return lax.ppermute(value, AXES, pairs_of(move))


def after(value, *earlier):
    return lax.optimization_barrier((value, *earlier))[0]


class Order:
    def __init__(self, token):
        self.token = token

    def wait(self, *values):
        *values, self.token = lax.optimization_barrier((*values, self.token))
        return values if len(values) > 1 else values[0]

    def run(self, operation, *values):
        *values, self.token = lax.optimization_barrier((*values, self.token))
        found = operation(*values)
        return self.wait(*found) if isinstance(found, (list, tuple)) else self.wait(found)


def to_core(y, z, x, c):
    return (y, z, x, 1 - c)


def to_x(y, z, x, c):
    return (y, z, 1 - x, c)


def to_y(y, z, x, c):
    return (1 - y, z, x, c)


def to_first(y, z, x, c):
    return to_x(y, z, x, c) if c == 0 else to_y(y, z, x, c)


def to_second(y, z, x, c):
    return to_y(y, z, x, c) if c == 0 else to_x(y, z, x, c)


def to_corner(y, z, x, c):
    return to_x(y, z, x, c) if c == 0 else to_y(y, z, x, c)


def to_z(steps):
    return lambda y, z, x, c: (y, steps[z], x, c) if z in steps else None


Z_ONE = to_z({0: 1, 1: 0, 2: 3, 3: 2})
Z_IN = to_z({0: 1, 3: 2})
Z_MIDDLE = to_z({1: 2, 2: 1})
Z_OUT = to_z({1: 0, 2: 3})


VMEM = pl.BlockSpec(memory_space=pltpu.VMEM)
SMEM = pl.BlockSpec(memory_space=pltpu.SMEM)


def call(kernel, outs, scalars, *operands, name, cost=3 * 10**6, aliases=None):
    return pl.pallas_call(
        kernel,
        out_shape=outs,
        in_specs=[SMEM] + [VMEM] * len(operands),
        out_specs=jax.tree.map(lambda _: VMEM, outs),
        input_output_aliases=aliases or {},
        cost_estimate=pl.CostEstimate(flops=100 * cost, bytes_accessed=cost, transcendentals=0),
        compiler_params=pltpu.CompilerParams(vmem_limit_bytes=24 * 2**20),
        name=name,
    )(jnp.stack(scalars).astype(jnp.int32), *operands)


def dot(left, right):
    return jnp.dot(left, right, preferred_element_type=jnp.float32)


def halves(tokens):
    half = tokens.shape[0] // 2
    return pl.ds(0, half), pl.ds(half, half)


def partials(block, x, core, heres, theres, tokens_ref, leave, out_ref):
    depth = out_ref.shape[2]
    by_core = core == 0 if leave else core != 0
    place_fixed, place_by_core = 1 - x if leave else x, jnp.where(by_core, x, 1 - x)
    fixed = [ref[...] for ref in (theres if leave else heres)]
    chosen = [jnp.where(by_core, there[...], here[...]) for here, there in zip(heres, theres)]
    order = (0, 1) if leave else (1, 0)
    for i, place, lefts in ((order[0], place_fixed, fixed), (order[1], place_by_core, chosen)):
        for begin in range(0, depth, 256):
            size = min(256, depth - begin)
            at = pl.ds(pl.multiple_of((2 * block + place) * depth, 128) + begin, size)
            total = sum(
                dot(left, tokens_ref[rows, at]) for left, rows in zip(lefts, halves(tokens_ref))
            )
            out_ref[i, :, pl.ds(begin, size)] = total.astype(out_ref.dtype)


def contract(scalars, depth, leave, tokens, *rights):
    def kernel(at_ref, tokens_ref, here_a, here_b, there_a, there_b, out_ref):
        place = at_ref[0], at_ref[1], at_ref[2]
        partials(*place, (here_a, here_b), (there_a, there_b), tokens_ref, leave, out_ref)

    dtype = jnp.bfloat16 if leave else jnp.float32
    out = jax.ShapeDtypeStruct((2, rights[0].shape[0], depth), dtype)
    return call(kernel, out, scalars, tokens, *rights, name="contract")


def turned_gradients(product_of, up_refs, column, gain, out_refs):
    head = gain.shape[1]
    for part, (up_ref, out_ref) in enumerate(zip(up_refs, out_refs)):
        half = up_ref.shape[0]
        for begin in range(0, half, 128):
            size = min(128, half - begin)
            within = pl.ds(begin, size)
            product = product_of(part, begin, size)
            weighted = up_ref[within, column].astype(jnp.float32) * gain
            pair = head_terms(product[:, :head], product[:, head:], weighted)
            for i, value in enumerate(pair):
                out_ref[pl.ds(i * head, head), within] = value.T.astype(jnp.bfloat16)


def side_column(at_ref, side, head):
    return pl.ds(pl.multiple_of((2 * side + at_ref[2]) * head, 128), head)


def gradients_here(scalars, own, first, second, upstream, other_up, norm_gain):
    half, width = own.shape[0] // 2, own.shape[1]
    head = norm_gain.shape[0]

    def kernel(at_ref, own_ref, first_ref, second_ref, up_a, up_b, gain_ref, *out_refs):
        own_first = at_ref[2] == 0

        def product_of(part, begin, size):
            at = pl.ds(part * half + begin, size)
            return own_ref[at, :] + jnp.where(own_first, first_ref[at, :], second_ref[at, :])

        column = side_column(at_ref, at_ref[3], head)
        turned_gradients(product_of, (up_a, up_b), column, gain_ref[...], out_refs)

    out = jax.ShapeDtypeStruct((width, half), jnp.bfloat16)
    operands = (own, first, second, upstream, other_up, norm_gain.reshape(1, head))
    return call(kernel, [out, out], scalars, *operands, name="gradients_here")


def gradients_there(scalars, tokens, heres, both, first, second, last, upstream, other_up, norm_gain):
    half, width = both.shape[0] // 2, both.shape[1]
    depth = last.shape[0]
    head = norm_gain.shape[0]

    def kernel(
        at_ref, tokens_ref, here_a, here_b, both_ref, first_ref, second_ref, last_ref, up_a, up_b, gain_ref,
        there_a, there_b, leaving_ref,
    ):
        block, x, core = at_ref[0], at_ref[1], at_ref[2]
        far = pl.ds(pl.multiple_of((2 * block + 1 - x) * depth, 128), depth)
        products = [dot(tokens_ref[rows, far], last_ref[...]) for rows in halves(tokens)]

        def product_of(part, begin, size):
            at = pl.ds(part * half + begin, size)
            by_core = jnp.where(core == 0, second_ref[at, :], first_ref[at, :])
            return both_ref[at, :] + by_core + products[part][begin : begin + size]

        column = side_column(at_ref, 1 - at_ref[3], head)
        turned_gradients(product_of, (up_a, up_b), column, gain_ref[...], (there_a, there_b))
        partials(
            block, x, core, (here_a, here_b), (there_a, there_b), tokens_ref, True, leaving_ref
        )

    out = jax.ShapeDtypeStruct((width, half), jnp.bfloat16)
    leaving = jax.ShapeDtypeStruct((2, width, depth), jnp.bfloat16)
    operands = (*heres, both, first, second, last, upstream, other_up, norm_gain.reshape(1, head))
    return call(kernel, [out, out, leaving], scalars, tokens, *operands, name="gradients_there")


def by_rows(scalars, *terms):
    width, depth = terms[0].shape
    half = depth // 2

    def kernel(at_ref, *refs):
        *term_refs, kept_ref, given_ref = refs

        def put(part, begin, value):
            rows = pl.ds(begin, value.shape[0])

            @pl.when(at_ref[2] == part)
            def _():
                kept_ref[rows, :] = value

            @pl.when(at_ref[2] != part)
            def _():
                given_ref[rows, :] = value.astype(given_ref.dtype)

        for begin in range(0, depth, 128):
            size = min(128, depth - begin)
            total = sum(ref[:, pl.ds(begin, size)].astype(jnp.float32) for ref in term_refs).T
            below = max(0, min(size, half - begin))
            if below:
                put(0, begin, total[:below])
            if below < size:
                put(1, begin + below - half, total[below:])

    outs = [jax.ShapeDtypeStruct((half, width), dtype) for dtype in (jnp.float32, jnp.bfloat16)]
    return call(kernel, outs, scalars, *terms, name="by_rows")


def finish(scalars, kept, taken, probe, momentum, curvature):
    head = kept.shape[1] // 2
    shares = momentum.shape[1] // head

    def kernel(at_ref, kept_ref, taken_ref, probe_ref, momentum_ref, curvature_ref, *out_refs):
        own_first = at_ref[0] == 0
        for i in range(shares):
            columns = pl.ds(i * head, head)
            mine = own_first if i == 0 else jnp.logical_not(own_first)
            share = jnp.where(mine, kept_ref[...], taken_ref[...].astype(jnp.float32))
            at = pl.multiple_of(at_ref[1] * (shares * head), 128) + i * head
            results = step_outputs(
                momentum_ref[:, columns],
                curvature_ref[:, columns],
                probe_ref[:, pl.ds(at, head)].astype(jnp.float32),
                share[:, :head],
                share[:, head:],
            )
            for out_ref, value in zip(out_refs, results):
                out_ref[:, columns] = value

    out = jax.ShapeDtypeStruct(momentum.shape, jnp.float32)
    return call(kernel, [out] * 3, scalars, kept, taken, probe, momentum, curvature, name="finish")


def unit_rows(scalars, head, weight, probe, units=()):
    rows = weight.shape[0]

    def kernel(at_ref, weight_ref, probe_ref, *refs):
        y, c = at_ref[0], at_ref[1]
        place = pl.ds(pl.multiple_of(at_ref[2] * rows, 16), rows)
        for side, out_ref in zip((y, 1 - y), refs[-2:]):
            column = pl.ds(pl.multiple_of((2 * side + c) * head, 128), head)
            for j, ref in enumerate((weight_ref, probe_ref)):
                out_ref[place, pl.ds(j * head, head)] = ref[:, column]

    out = jax.ShapeDtypeStruct((2 * rows, 2 * head), weight.dtype)
    aliases = {3: 0, 4: 1} if units else {}
    return call(kernel, [out, out], scalars, weight, probe, *units, name="unit_rows", aliases=aliases)


def by_links(acts, upstream, k_weight, probe, norm_gain, momentum, curvature):
    head = norm_gain.shape[0]
    rows = k_weight.shape[0]
    place = lax.axis_index("fsdp")
    y, z, x, c = lax.axis_index("dp"), place // 4, (place // 2) % 2, place % 2
    own_first = c == 0

    other_weight, other_probe = send(k_weight, to_core, "other_weight"), send(probe, to_core, "other_probe")
    own_rows = unit_rows((y, c, c), head, k_weight, probe)
    mine, beside = unit_rows((y, c, 1 - c), head, other_weight, other_probe, own_rows)
    other_up = send(upstream, to_core, "other_up")
    order = Order(momentum)
    other_acts = send(after(acts, mine), to_core, "other_acts")
    one = send(mine, Z_ONE, "one")
    near = send(mine, Z_MIDDLE, "near")
    across = send(mine, to_x, "across")
    other_up = order.wait(other_up)
    one, near = order.wait(one, near)
    two_out = send(near, Z_OUT, "two_out")
    two_in = send(one, Z_MIDDLE, "two_in")
    other_acts, one = order.wait(other_acts, one)
    one_first = send(one, to_first, "one_first")
    corner = order.run(lambda a, b: jnp.where(own_first, a, b), beside, across)
    corner = send(corner, to_corner, "corner")
    tokens = order.run(lambda a, b: jnp.concatenate([a, b], axis=0), acts, other_acts)

    def block_of(held, slot, flip_x):
        start = ((z ^ slot) * 2 + (x ^ flip_x)) * (2 * rows)
        return lax.dynamic_slice_in_dim(held, start, 2 * rows, 1)

    def add_product(total, slot, flip_x, unit):
        def product(unit, held, *before):
            found = jnp.dot(block_of(held, slot, flip_x), unit, preferred_element_type=jnp.float32)
            return sum(before, found)

        return order.run(product, unit, tokens, *(() if total is None else (total,)))

    own_sum = add_product(None, 0, 0, mine)
    both_sum = add_product(None, 0, 0, beside)
    own_sum = add_product(own_sum, 0, 1, across)
    two_out, two_in = order.wait(two_out, two_in)
    two = order.run(jnp.add, two_out, two_in)
    three_out = send(two, Z_OUT, "three_out")
    own_sum = add_product(own_sum, 1, 0, one)
    one_first = order.wait(one_first)
    one_both = send(one_first, to_second, "one_both")
    corner, two = order.wait(corner, two)
    two_first = send(two, to_first, "two_first")
    two_second = send(two, to_second, "two_second")
    both_sum = add_product(both_sum, 0, 1, corner)
    first_sum = add_product(None, 1, 1 - c, one_first)
    own_sum = add_product(own_sum, 2, 0, two)
    three = order.run(jnp.add, near, three_out)
    three_first = send(three, to_first, "three_first")
    flip = order.run(lambda a, b: jnp.where(own_first, a, b), beside, across)
    one_second = send(flip, Z_ONE, "one_second")
    three_second = send(three, to_second, "three_second")
    two_first = order.wait(two_first)
    two_both = send(two_first, to_second, "two_both")
    both_sum = add_product(both_sum, 1, 1, one_both)
    first_sum = add_product(first_sum, 2, 1 - c, two_first)
    own_sum = add_product(own_sum, 3, 0, three)
    second_sum = add_product(None, 2, c, two_second)
    three_first = order.wait(three_first)
    three_both = send(three_first, to_second, "three_both")
    first_sum = add_product(first_sum, 3, 1 - c, three_first)
    both_sum = add_product(both_sum, 2, 1, two_both)
    second_sum = add_product(second_sum, 1, c, one_second)
    second_sum = add_product(second_sum, 3, c, three_second)
    place = (z ^ 3, x, c, y)
    ups = (upstream, other_up, norm_gain)
    heres = order.run(
        lambda *sums: gradients_here(place, *sums, *ups), own_sum, first_sum, second_sum
    )
    *theres, leaving_3 = gradients_there(
        place, tokens, heres, both_sum, first_sum, second_sum, order.wait(three_both), *ups
    )

    def partial(slot, leave):
        def product(*operands):
            return contract((z ^ slot, x, c), 2 * rows, leave, *operands)

        return order.run(product, tokens, *heres, *theres)

    def total_of(*terms):
        return sum((t.astype(jnp.float32) for t in terms[1:]), terms[0].astype(jnp.float32))

    def rounded(part, kept, got, *more):
        def total(kept, got, *more):
            return total_of(kept[part], got[part], *more).astype(jnp.bfloat16)

        return order.run(total, kept, got, *more)

    def sum_of(*terms):
        return order.run(lambda *t: total_of(*t).astype(jnp.bfloat16), *terms)

    seconds_3 = send(leaving_3, to_second, "seconds_3")
    raw_1 = send(partial(1, True), Z_ONE, "raw_1")
    seconds_2 = send(partial(2, True), to_second, "seconds_2")
    kept_3 = partial(3, False)
    first_3 = send(rounded(0, kept_3, seconds_3), to_first, "first_3")
    leaving_0 = partial(0, True)
    kept_2 = partial(2, False)
    kept_1 = partial(1, False)
    kept_0 = partial(0, False)
    leaving_0 = sum_of(leaving_0, raw_1)
    sum_3 = rounded(1, kept_3, seconds_3, first_3)
    three_in = send(sum_3, Z_IN, "three_in")
    first_2 = send(rounded(0, kept_2, seconds_2), to_first, "first_2")
    first_1 = send(order.run(lambda kept: kept[0].astype(jnp.bfloat16), kept_1), to_first, "first_1")
    leaving_0 = order.wait(leaving_0)
    seconds_0 = send(leaving_0, to_second, "seconds_0")
    sum_2 = rounded(1, kept_2, seconds_2, first_2, three_in)
    two_in = send(sum_2, Z_IN, "two_in")
    two = send(sum_2, Z_MIDDLE, "two")
    own_1 = order.run(lambda kept, got: total_of(kept[1], got), kept_1, first_1)
    first_0 = send(rounded(0, kept_0, seconds_0), to_first, "first_0")
    three = send(sum_of(sum_3, two_in), Z_MIDDLE, "three")
    one = send(sum_of(own_1, two), Z_ONE, "one")
    own_0 = order.run(lambda kept, got: total_of(kept[1], got[1]), kept_0, seconds_0)

    def turned(*terms):
        return by_rows((y, x, c), *terms)

    kept, given = order.run(turned, own_0, first_0, three, one)
    taken = send(given, to_core, "taken")
    return tuple(finish((c, y), kept, taken, probe, order.token, curvature))


def solution(mesh):
    on_links = mesh.shape["dp"] == 2 and mesh.shape["fsdp"] == 16
    return jax.shard_map(
        by_links if on_links else by_collectives,
        mesh=mesh,
        in_specs=(
            P(("dp", "fsdp"), None),
            P(("dp", "fsdp"), None),
            P("fsdp", None),
            P("fsdp", None),
            P(),
            P("fsdp", "dp"),
            P("fsdp", "dp"),
        ),
        out_specs=(P("fsdp", "dp"), P("fsdp", "dp"), P("fsdp", "dp")),
        check_vma=False,
    )
```

```python
import functools

import jax
import jax.numpy as jnp
from jax import lax
from jax.experimental import pallas as pl
from jax.experimental.pallas import tpu as pltpu
from jax.sharding import PartitionSpec as P

AXES = ("dp", "fsdp")


def contract_tokens(left, right):
    return lax.dot_general(
        left, right, (((0,), (0,)), ((), ())), preferred_element_type=jnp.float32
    )


def head_terms(values, moving, weighted):
    head_size = values.shape[-1]
    inverse = lax.rsqrt(jnp.mean(values * values, axis=-1, keepdims=True) + 1e-06)
    cubed = inverse * inverse * inverse
    along = jnp.sum(weighted * values, axis=-1, keepdims=True)
    grad_vals = inverse * weighted - cubed * values * along / head_size
    inverse_dot = -cubed * jnp.sum(values * moving, axis=-1, keepdims=True) / head_size
    along_dot = jnp.sum(weighted * moving, axis=-1, keepdims=True)
    hvp_vals = (
        inverse_dot * weighted
        - (
            3.0 * inverse * inverse * inverse_dot * values * along
            + cubed * moving * along
            + cubed * values * along_dot
        )
        / head_size
    )
    return grad_vals, hvp_vals


def step_outputs(momentum, curvature, probe_cols, grad_share, hvp_share):
    new_momentum = 0.965 * momentum + 0.035 * grad_share
    new_curvature = 0.99 * curvature + 0.01 * (probe_cols * hvp_share)
    update = jnp.clip(new_momentum / jnp.maximum(0.5 * new_curvature, 0.25), -1.0, 1.0)
    return (new_momentum, new_curvature, update)


def by_collectives(acts, upstream, k_weight, probe, norm_gain, momentum, curvature):
    width = k_weight.shape[1]
    weight_piece = lax.all_gather(k_weight, "fsdp", axis=0, tiled=True)
    probe_piece = lax.all_gather(probe, "fsdp", axis=0, tiled=True)
    projected = jnp.dot(acts, weight_piece, preferred_element_type=jnp.float32)
    tangent = jnp.dot(acts, probe_piece, preferred_element_type=jnp.float32)
    shaped = (acts.shape[0], -1, norm_gain.shape[0])
    weighted = upstream.astype(jnp.float32).reshape(shaped) * norm_gain
    pair = head_terms(projected.reshape(shaped), tangent.reshape(shaped), weighted)
    stacked = jnp.concatenate([v.reshape(acts.shape[0], -1) for v in pair], axis=1)
    owned = lax.psum_scatter(
        contract_tokens(acts, stacked.astype(jnp.bfloat16)).astype(jnp.bfloat16),
        "fsdp",
        scatter_dimension=0,
        tiled=True,
    ).astype(jnp.float32)
    grad_share, hvp_share = (
        lax.psum_scatter(owned[:, :width], "dp", scatter_dimension=1, tiled=True),
        lax.psum_scatter(owned[:, width:], "dp", scatter_dimension=1, tiled=True),
    )
    share_width = grad_share.shape[1]
    probe_cols = lax.dynamic_slice_in_dim(
        probe, lax.axis_index("dp") * share_width, share_width, 1
    ).astype(jnp.float32)
    return step_outputs(momentum, curvature, probe_cols, grad_share, hvp_share)


def pairs_of(move):
    def flat(y, z, x, c):
        return ((y * 4 + z) * 2 + x) * 2 + c

    found = []
    for y in range(2):
        for z in range(4):
            for x in range(2):
                for c in range(2):
                    target = move(y, z, x, c)
                    if target is not None:
                        found.append((flat(y, z, x, c), flat(*target)))
    return found


def send(value, move, name="exchange"):
    with jax.named_scope(name):
        return lax.ppermute(value, AXES, pairs_of(move))


def after(value, *earlier):
    return lax.optimization_barrier((value, *earlier))[0]


class Order:
    def __init__(self, token):
        self.token = token

    def wait(self, *values):
        *values, self.token = lax.optimization_barrier((*values, self.token))
        return values if len(values) > 1 else values[0]

    def run(self, operation, *values):
        *values, self.token = lax.optimization_barrier((*values, self.token))
        found = operation(*values)
        return self.wait(*found) if isinstance(found, (list, tuple)) else self.wait(found)


def to_core(y, z, x, c):
    return (y, z, x, 1 - c)


def to_x(y, z, x, c):
    return (y, z, 1 - x, c)


def to_y(y, z, x, c):
    return (1 - y, z, x, c)


def to_first(y, z, x, c):
    return to_x(y, z, x, c) if c == 0 else to_y(y, z, x, c)


def to_second(y, z, x, c):
    return to_y(y, z, x, c) if c == 0 else to_x(y, z, x, c)


def to_corner(y, z, x, c):
    return to_x(y, z, x, c) if c == 0 else to_y(y, z, x, c)


def to_z(steps):
    return lambda y, z, x, c: (y, steps[z], x, c) if z in steps else None


Z_ONE = to_z({0: 1, 1: 0, 2: 3, 3: 2})
Z_IN = to_z({0: 1, 3: 2})
Z_MIDDLE = to_z({1: 2, 2: 1})
Z_OUT = to_z({1: 0, 2: 3})


VMEM = pl.BlockSpec(memory_space=pltpu.VMEM)
SMEM = pl.BlockSpec(memory_space=pltpu.SMEM)


def call(kernel, outs, scalars, *operands, name, cost=10**6, aliases=None):
    return pl.pallas_call(
        kernel,
        out_shape=outs,
        in_specs=[SMEM] + [VMEM] * len(operands),
        out_specs=jax.tree.map(lambda _: VMEM, outs),
        input_output_aliases=aliases or {},
        cost_estimate=pl.CostEstimate(flops=100 * cost, bytes_accessed=cost, transcendentals=0),
        compiler_params=pltpu.CompilerParams(vmem_limit_bytes=24 * 2**20),
        name=name,
    )(jnp.stack(scalars).astype(jnp.int32), *operands)


def dot(left, right):
    return jnp.dot(left, right, preferred_element_type=jnp.float32)


def halves(tokens):
    half = tokens.shape[0] // 2
    return pl.ds(0, half), pl.ds(half, half)


def partials(block, x, core, heres, theres, tokens_ref, leave, out_ref):
    depth = out_ref.shape[2]
    by_core = core == 0 if leave else core != 0
    place_fixed, place_by_core = 1 - x if leave else x, jnp.where(by_core, x, 1 - x)
    fixed = [ref[...] for ref in (theres if leave else heres)]
    chosen = [jnp.where(by_core, there[...], here[...]) for here, there in zip(heres, theres)]
    order = (0, 1) if leave else (1, 0)
    for i, place, lefts in ((order[0], place_fixed, fixed), (order[1], place_by_core, chosen)):
        for begin in range(0, depth, 256):
            size = min(256, depth - begin)
            at = pl.ds(pl.multiple_of((2 * block + place) * depth, 128) + begin, size)
            total = sum(
                dot(left, tokens_ref[rows, at]) for left, rows in zip(lefts, halves(tokens_ref))
            )
            out_ref[i, :, pl.ds(begin, size)] = total.astype(out_ref.dtype)


def contract(scalars, depth, leave, tokens, *rights):
    def kernel(at_ref, tokens_ref, here_a, here_b, there_a, there_b, out_ref):
        place = at_ref[0], at_ref[1], at_ref[2]
        partials(*place, (here_a, here_b), (there_a, there_b), tokens_ref, leave, out_ref)

    dtype = jnp.bfloat16 if leave else jnp.float32
    out = jax.ShapeDtypeStruct((2, rights[0].shape[0], depth), dtype)
    return call(kernel, out, scalars, tokens, *rights, name="contract")


def turned_gradients(product_of, up_refs, column, gain, out_refs):
    head = gain.shape[1]
    for part, (up_ref, out_ref) in enumerate(zip(up_refs, out_refs)):
        half = up_ref.shape[0]
        for begin in range(0, half, 128):
            size = min(128, half - begin)
            within = pl.ds(begin, size)
            product = product_of(part, begin, size)
            weighted = up_ref[within, column].astype(jnp.float32) * gain
            pair = head_terms(product[:, :head], product[:, head:], weighted)
            for i, value in enumerate(pair):
                out_ref[pl.ds(i * head, head), within] = value.T.astype(jnp.bfloat16)


def side_column(at_ref, side, head):
    return pl.ds(pl.multiple_of((2 * side + at_ref[2]) * head, 128), head)


def gradients_here(scalars, own, first, second, upstream, other_up, norm_gain):
    half, width = own.shape[0] // 2, own.shape[1]
    head = norm_gain.shape[0]

    def kernel(at_ref, own_ref, first_ref, second_ref, up_a, up_b, gain_ref, *out_refs):
        own_first = at_ref[2] == 0

        def product_of(part, begin, size):
            at = pl.ds(part * half + begin, size)
            return own_ref[at, :] + jnp.where(own_first, first_ref[at, :], second_ref[at, :])

        column = side_column(at_ref, at_ref[3], head)
        turned_gradients(product_of, (up_a, up_b), column, gain_ref[...], out_refs)

    out = jax.ShapeDtypeStruct((width, half), jnp.bfloat16)
    operands = (own, first, second, upstream, other_up, norm_gain.reshape(1, head))
    return call(kernel, [out, out], scalars, *operands, name="gradients_here")


def gradients_there(scalars, tokens, heres, both, first, second, last, upstream, other_up, norm_gain):
    half, width = both.shape[0] // 2, both.shape[1]
    depth = last.shape[0]
    head = norm_gain.shape[0]

    def kernel(
        at_ref, tokens_ref, here_a, here_b, both_ref, first_ref, second_ref, last_ref, up_a, up_b, gain_ref,
        there_a, there_b, leaving_ref,
    ):
        block, x, core = at_ref[0], at_ref[1], at_ref[2]
        far = pl.ds(pl.multiple_of((2 * block + 1 - x) * depth, 128), depth)
        products = [dot(tokens_ref[rows, far], last_ref[...]) for rows in halves(tokens)]

        def product_of(part, begin, size):
            at = pl.ds(part * half + begin, size)
            by_core = jnp.where(core == 0, second_ref[at, :], first_ref[at, :])
            return both_ref[at, :] + by_core + products[part][begin : begin + size]

        column = side_column(at_ref, 1 - at_ref[3], head)
        turned_gradients(product_of, (up_a, up_b), column, gain_ref[...], (there_a, there_b))
        partials(
            block, x, core, (here_a, here_b), (there_a, there_b), tokens_ref, True, leaving_ref
        )

    out = jax.ShapeDtypeStruct((width, half), jnp.bfloat16)
    leaving = jax.ShapeDtypeStruct((2, width, depth), jnp.bfloat16)
    operands = (*heres, both, first, second, last, upstream, other_up, norm_gain.reshape(1, head))
    return call(kernel, [out, out, leaving], scalars, tokens, *operands, name="gradients_there")


def by_rows(scalars, *terms):
    width, depth = terms[0].shape
    half = depth // 2

    def kernel(at_ref, *refs):
        *term_refs, kept_ref, given_ref = refs

        def put(part, begin, value):
            rows = pl.ds(begin, value.shape[0])

            @pl.when(at_ref[2] == part)
            def _():
                kept_ref[rows, :] = value

            @pl.when(at_ref[2] != part)
            def _():
                given_ref[rows, :] = value.astype(given_ref.dtype)

        for begin in range(0, depth, 128):
            size = min(128, depth - begin)
            total = sum(ref[:, pl.ds(begin, size)].astype(jnp.float32) for ref in term_refs).T
            below = max(0, min(size, half - begin))
            if below:
                put(0, begin, total[:below])
            if below < size:
                put(1, begin + below - half, total[below:])

    outs = [jax.ShapeDtypeStruct((half, width), dtype) for dtype in (jnp.float32, jnp.bfloat16)]
    return call(kernel, outs, scalars, *terms, name="by_rows")


def finish(scalars, kept, taken, probe, momentum, curvature):
    head = kept.shape[1] // 2
    shares = momentum.shape[1] // head

    def kernel(at_ref, kept_ref, taken_ref, probe_ref, momentum_ref, curvature_ref, *out_refs):
        own_first = at_ref[0] == 0
        for i in range(shares):
            columns = pl.ds(i * head, head)
            mine = own_first if i == 0 else jnp.logical_not(own_first)
            share = jnp.where(mine, kept_ref[...], taken_ref[...].astype(jnp.float32))
            at = pl.multiple_of(at_ref[1] * (shares * head), 128) + i * head
            results = step_outputs(
                momentum_ref[:, columns],
                curvature_ref[:, columns],
                probe_ref[:, pl.ds(at, head)].astype(jnp.float32),
                share[:, :head],
                share[:, head:],
            )
            for out_ref, value in zip(out_refs, results):
                out_ref[:, columns] = value

    out = jax.ShapeDtypeStruct(momentum.shape, jnp.float32)
    return call(kernel, [out] * 3, scalars, kept, taken, probe, momentum, curvature, name="finish")


def unit_rows(scalars, head, weight, probe, units=()):
    rows = weight.shape[0]

    def kernel(at_ref, weight_ref, probe_ref, *refs):
        y, c = at_ref[0], at_ref[1]
        place = pl.ds(pl.multiple_of(at_ref[2] * rows, 16), rows)
        for side, out_ref in zip((y, 1 - y), refs[-2:]):
            column = pl.ds(pl.multiple_of((2 * side + c) * head, 128), head)
            for j, ref in enumerate((weight_ref, probe_ref)):
                out_ref[place, pl.ds(j * head, head)] = ref[:, column]

    out = jax.ShapeDtypeStruct((2 * rows, 2 * head), weight.dtype)
    aliases = {3: 0, 4: 1} if units else {}
    return call(kernel, [out, out], scalars, weight, probe, *units, name="unit_rows", aliases=aliases)


def by_links(acts, upstream, k_weight, probe, norm_gain, momentum, curvature):
    head = norm_gain.shape[0]
    rows = k_weight.shape[0]
    place = lax.axis_index("fsdp")
    y, z, x, c = lax.axis_index("dp"), place // 4, (place // 2) % 2, place % 2
    own_first = c == 0

    other_weight, other_probe = send(k_weight, to_core, "other_weight"), send(probe, to_core, "other_probe")
    own_rows = unit_rows((y, c, c), head, k_weight, probe)
    mine, beside = unit_rows((y, c, 1 - c), head, other_weight, other_probe, own_rows)
    other_up = send(upstream, to_core, "other_up")
    order = Order(momentum)
    other_acts = send(after(acts, mine), to_core, "other_acts")
    one = send(mine, Z_ONE, "one")
    near = send(mine, Z_MIDDLE, "near")
    across = send(mine, to_x, "across")
    other_up = order.wait(other_up)
    one, near = order.wait(one, near)
    two_out = send(near, Z_OUT, "two_out")
    two_in = send(one, Z_MIDDLE, "two_in")
    other_acts, one = order.wait(other_acts, one)
    one_first = send(one, to_first, "one_first")
    corner = order.run(lambda a, b: jnp.where(own_first, a, b), beside, across)
    corner = send(corner, to_corner, "corner")
    tokens = order.run(lambda a, b: jnp.concatenate([a, b], axis=0), acts, other_acts)

    def block_of(held, slot, flip_x):
        start = ((z ^ slot) * 2 + (x ^ flip_x)) * (2 * rows)
        return lax.dynamic_slice_in_dim(held, start, 2 * rows, 1)

    def add_product(total, slot, flip_x, unit):
        def product(unit, held, *before):
            found = jnp.dot(block_of(held, slot, flip_x), unit, preferred_element_type=jnp.float32)
            return sum(before, found)

        return order.run(product, unit, tokens, *(() if total is None else (total,)))

    own_sum = add_product(None, 0, 0, mine)
    both_sum = add_product(None, 0, 0, beside)
    own_sum = add_product(own_sum, 0, 1, across)
    two_out, two_in = order.wait(two_out, two_in)
    two = order.run(jnp.add, two_out, two_in)
    three_out = send(two, Z_OUT, "three_out")
    own_sum = add_product(own_sum, 1, 0, one)
    one_first = order.wait(one_first)
    one_both = send(one_first, to_second, "one_both")
    corner, two = order.wait(corner, two)
    two_first = send(two, to_first, "two_first")
    two_second = send(two, to_second, "two_second")
    both_sum = add_product(both_sum, 0, 1, corner)
    first_sum = add_product(None, 1, 1 - c, one_first)
    own_sum = add_product(own_sum, 2, 0, two)
    three = order.run(jnp.add, near, three_out)
    three_first = send(three, to_first, "three_first")
    flip = order.run(lambda a, b: jnp.where(own_first, a, b), beside, across)
    one_second = send(flip, Z_ONE, "one_second")
    three_second = send(three, to_second, "three_second")
    two_first = order.wait(two_first)
    two_both = send(two_first, to_second, "two_both")
    both_sum = add_product(both_sum, 1, 1, one_both)
    first_sum = add_product(first_sum, 2, 1 - c, two_first)
    own_sum = add_product(own_sum, 3, 0, three)
    second_sum = add_product(None, 2, c, two_second)
    three_first = order.wait(three_first)
    three_both = send(three_first, to_second, "three_both")
    first_sum = add_product(first_sum, 3, 1 - c, three_first)
    both_sum = add_product(both_sum, 2, 1, two_both)
    second_sum = add_product(second_sum, 1, c, one_second)
    second_sum = add_product(second_sum, 3, c, three_second)
    place = (z ^ 3, x, c, y)
    ups = (upstream, other_up, norm_gain)
    heres = order.run(
        lambda *sums: gradients_here(place, *sums, *ups), own_sum, first_sum, second_sum
    )
    *theres, leaving_3 = gradients_there(
        place, tokens, heres, both_sum, first_sum, second_sum, order.wait(three_both), *ups
    )

    def partial(slot, leave):
        def product(*operands):
            return contract((z ^ slot, x, c), 2 * rows, leave, *operands)

        return order.run(product, tokens, *heres, *theres)

    def total_of(*terms):
        return sum((t.astype(jnp.float32) for t in terms[1:]), terms[0].astype(jnp.float32))

    def rounded(part, kept, got, *more):
        def total(kept, got, *more):
            return total_of(kept[part], got[part], *more).astype(jnp.bfloat16)

        return order.run(total, kept, got, *more)

    def sum_of(*terms):
        return order.run(lambda *t: total_of(*t).astype(jnp.bfloat16), *terms)

    seconds_3 = send(leaving_3, to_second, "seconds_3")
    raw_1 = send(partial(1, True), Z_ONE, "raw_1")
    seconds_2 = send(partial(2, True), to_second, "seconds_2")
    kept_3 = partial(3, False)
    first_3 = send(rounded(0, kept_3, seconds_3), to_first, "first_3")
    leaving_0 = partial(0, True)
    kept_2 = partial(2, False)
    kept_1 = partial(1, False)
    kept_0 = partial(0, False)
    leaving_0 = sum_of(leaving_0, raw_1)
    sum_3 = rounded(1, kept_3, seconds_3, first_3)
    three_in = send(sum_3, Z_IN, "three_in")
    first_2 = send(rounded(0, kept_2, seconds_2), to_first, "first_2")
    first_1 = send(order.run(lambda kept: kept[0].astype(jnp.bfloat16), kept_1), to_first, "first_1")
    leaving_0 = order.wait(leaving_0)
    seconds_0 = send(leaving_0, to_second, "seconds_0")
    sum_2 = rounded(1, kept_2, seconds_2, first_2, three_in)
    two_in = send(sum_2, Z_IN, "two_in")
    two = send(sum_2, Z_MIDDLE, "two")
    own_1 = order.run(lambda kept, got: total_of(kept[1], got), kept_1, first_1)
    first_0 = send(rounded(0, kept_0, seconds_0), to_first, "first_0")
    three = send(sum_of(sum_3, two_in), Z_MIDDLE, "three")
    one = send(sum_of(own_1, two), Z_ONE, "one")
    own_0 = order.run(lambda kept, got: total_of(kept[1], got[1]), kept_0, seconds_0)

    def turned(*terms):
        return by_rows((y, x, c), *terms)

    kept, given = order.run(turned, own_0, first_0, three, one)
    taken = send(given, to_core, "taken")
    return tuple(finish((c, y), kept, taken, probe, order.token, curvature))


def solution(mesh):
    on_links = mesh.shape["dp"] == 2 and mesh.shape["fsdp"] == 16
    return jax.shard_map(
        by_links if on_links else by_collectives,
        mesh=mesh,
        in_specs=(
            P(("dp", "fsdp"), None),
            P(("dp", "fsdp"), None),
            P("fsdp", None),
            P("fsdp", None),
            P(),
            P("fsdp", "dp"),
            P("fsdp", "dp"),
        ),
        out_specs=(P("fsdp", "dp"), P("fsdp", "dp"), P("fsdp", "dp")),
        check_vma=False,
    )
```
